256 devices in a mesh: row: 8 (over y_lo, x), col: 32 (over y_hi, z, core).
Axes of the slice: x: 4, y: 4 (y_hi: 2, y_lo: 2; y = y_hi * 2 + y_lo), z: 8, core: 2. Of those that a mesh axis runs over, the one named last changes fastest.
Arguments:
- p_blocks: bfloat16 [8, 3, 256, 128, 128], P('row', None, 'col'), may hold values from -1.1953125 to 1.1953125
- p_rows: int32 [8, 3, 256], P('row', None, 'col'), may hold values from -1 to 31, as said below
- c_rows: int32 [8, 3, 256], P('row', None, 'col'), may hold values from 0 to 31, as said below
Outputs:
- c_blocks: float32 [8, 3, 256, 128, 128], P('row', None, 'col')
The draws below stay inside these ranges and needn't reach their ends.
Inputs may be any that keep to these rules, and one draw needn't show every extreme that they name: `p_rows`: -1 marks an empty slot, whose block in p_blocks is not part of P; the block rows named in one block column of one grid row are distinct; one device's 8 block columns of one grid row hold at most 16 stored blocks, and exactly that many on some device; of one device's stored blocks, at most 6 lie in any one aligned range of 8 block rows (rows m * 8 to m * 8 + 7 of the grid row), and exactly that many on some device. `c_rows`: the 3 block rows named in one block column of one grid row are distinct.
All inputs are finite; a program needn't handle non-finite values.
Results may differ from the reference program's by a relative error of at most 0.0003.
Values may be sent and summed in bfloat16 or wider, within the bound.
A program may use at most 64 MiB of HBM per device.

```python
import jax
import jax.numpy as jnp
from jax import lax

BLK = 128
BC_DEV = 8
CK = 3
CR = 3
SECTIONS = 4
ROW_GRID = 8
COL_GRID = 32
NBLK = 256
BR_DEV = 32
NNZ_DEV = 16


def block_pattern(key):
    key_rows, key_count, key_full, key_rank, key_favor = jax.random.split(key, 5)
    tile_count = ROW_GRID * COL_GRID
    slot_count = CK * BC_DEV
    ranges = BR_DEV // BC_DEV
    column_keys = jax.random.split(key_rows, ROW_GRID * NBLK)
    within_perm = jax.vmap(lambda sub_key: jax.random.permutation(sub_key, BC_DEV))(column_keys)
    within_perm = within_perm.reshape(ROW_GRID, NBLK, BC_DEV).astype(jnp.int32)
    slot_iota = jnp.arange(CK, dtype=jnp.int32)
    local_col = jnp.arange(NBLK, dtype=jnp.int32) % BC_DEV
    segment = (slot_iota[:, None] + local_col[None, :]) % ranges
    within = within_perm[:, :, slot_iota // ranges].transpose(0, 2, 1)
    chosen = (segment[None] * BC_DEV + within).astype(jnp.int32)
    counts = jax.random.randint(key_count, (tile_count,), NNZ_DEV // 2, NNZ_DEV + 1)
    fullest = jax.random.randint(key_full, (), 0, tile_count)
    favored = jax.random.randint(key_favor, (), 0, ranges)
    counts = jnp.where(jnp.arange(tile_count) == fullest, NNZ_DEV, counts)
    ranks = jax.vmap(lambda sub_key: jax.random.permutation(sub_key, slot_count))(jax.random.split(key_rank, tile_count))
    tile_segment = ((slot_iota[:, None] + jnp.arange(BC_DEV, dtype=jnp.int32)[None, :]) % ranges).reshape(slot_count)
    is_full = jnp.arange(tile_count) == fullest
    scores = ranks + jnp.where(is_full[:, None] & (tile_segment[None, :] != favored), slot_count, 0)
    position = jnp.argsort(jnp.argsort(scores, axis=1), axis=1)
    valid = position < counts[:, None]
    valid = valid.reshape(ROW_GRID, COL_GRID, CK, BC_DEV).transpose(0, 2, 1, 3).reshape(ROW_GRID, CK, NBLK)
    return jnp.where(valid, chosen, -1).astype(jnp.int32)


def draw_p_rows(key, part):
    pattern_rows = block_pattern(key)
    return pattern_rows


def draw_c_rows(key, part):
    pattern_rows = block_pattern(key)
    key = jax.random.fold_in(key, 7)
    hit_count = jnp.zeros((ROW_GRID, NBLK, BR_DEV), jnp.int32)
    iota_rows = jnp.arange(BR_DEV, dtype=jnp.int32)
    for section_num in range(SECTIONS):
        panel_col = section_num * (COL_GRID // SECTIONS)
        root_row = panel_col * BC_DEV // BR_DEV
        offset = panel_col * BC_DEV % BR_DEV
        b_rows = pattern_rows[root_row]
        in_panel = b_rows - offset
        b_live = (b_rows >= 0) & (in_panel >= 0) & (in_panel < BC_DEV)
        a_column = panel_col * BC_DEV + jnp.clip(in_panel, 0, BC_DEV - 1)
        a_rows = pattern_rows[:, :, a_column]
        found = (a_rows[..., None] == iota_rows) & b_live[None, None, :, :, None]
        hit_count = hit_count + jnp.sum(found.astype(jnp.int32), axis=(1, 2))
    ranks = jax.vmap(lambda sub_key: jax.random.permutation(sub_key, BR_DEV))(jax.random.split(key, ROW_GRID * NBLK))
    scores = jnp.minimum(hit_count, 1) * BR_DEV + ranks.reshape(ROW_GRID, NBLK, BR_DEV).astype(jnp.int32)
    unused, picked = lax.top_k(scores, CR)
    return picked.transpose(0, 2, 1).astype(jnp.int32)


def level_of(stream_key, shape, cuts, least, high):
    loudness, own = 1.0, jax.random.fold_in(stream_key, 6)
    for dim, parts in cuts:
        steps = jnp.exp(jax.random.uniform(jax.random.fold_in(own, dim), (parts,), jnp.float32, least / len(cuts), high / len(cuts)))
        loudness = loudness * jnp.repeat(steps, shape[dim] // parts).reshape([-1 if axis == dim else 1 for axis in range(len(shape))])
    return loudness


def noise(own_key, extent, deviation, limit, shards=(), kind=jnp.bfloat16):
    level = level_of(own_key, extent, shards, -0.22, 0.18) if shards else 1.0
    drawn = jax.random.normal(own_key, extent, jnp.float32) * deviation * level
    return jnp.minimum(jnp.maximum(drawn, -limit), limit).astype(kind)


def setup_inputs(seed: int = 0) -> dict:
    arg_keys = jax.random.split(jax.random.key(seed), 4)
    p_blocks = noise(arg_keys[0], (ROW_GRID, CK, NBLK, BLK, BLK), 0.2, 1.1953125, ((0, 8), (2, 32)))
    p_rows = draw_p_rows(jax.random.fold_in(arg_keys[3], 71), 0)
    c_rows = draw_c_rows(jax.random.fold_in(arg_keys[3], 71), 0)
    return {"p_blocks": p_blocks, "p_rows": p_rows, "c_rows": c_rows}


def section_terms(a_blocks, a_rows, b_blocks, b_rows, targets, offset):
    col_count = a_rows.shape[1]
    in_panel = b_rows - offset
    b_live = (b_rows >= 0) & (in_panel >= 0) & (in_panel < col_count)
    in_panel = jnp.clip(in_panel, 0, col_count - 1).astype(jnp.int32)
    picked_rows = a_rows[:, in_panel]
    picked = a_blocks[:, in_panel].astype(jnp.float32)
    matches = (picked_rows[:, None] == targets[None, :, None, :]) & b_live[None, None]
    selected = jnp.sum(jnp.where(matches[..., None, None], picked[:, None], jnp.zeros((), jnp.float32)), axis=0)
    return jnp.einsum('rejxy,ejyz->rjxz', selected, b_blocks.astype(jnp.float32), precision=lax.Precision.HIGHEST)


def reference(p_blocks, p_rows, c_rows):
    stride = COL_GRID // SECTIONS

    def row_tiles(row_pos):
        grid_blocks = p_blocks[row_pos]
        grid_rows = p_rows[row_pos]
        grid_targets = c_rows[row_pos]

        def one_tile(col_pos):
            start = (col_pos * BC_DEV).astype(jnp.int32)
            targets = lax.dynamic_slice_in_dim(grid_targets, start, BC_DEV, 1)
            running = jnp.zeros((CR, BC_DEV, BLK, BLK), jnp.float32)
            for section_num in range(SECTIONS):
                panel_col = section_num * stride
                root_row = panel_col * BC_DEV // BR_DEV
                offset = panel_col * BC_DEV % BR_DEV
                a_blocks = grid_blocks[:, panel_col * BC_DEV:(panel_col + 1) * BC_DEV]
                a_rows = grid_rows[:, panel_col * BC_DEV:(panel_col + 1) * BC_DEV]
                b_blocks = lax.dynamic_slice_in_dim(p_blocks[root_row], start, BC_DEV, 1)
                b_rows = lax.dynamic_slice_in_dim(p_rows[root_row], start, BC_DEV, 1)
                running = running + section_terms(a_blocks, a_rows, b_blocks, b_rows, targets, offset)
            return running

        tiles = lax.map(one_tile, jnp.arange(COL_GRID, dtype=jnp.int32))
        return tiles.transpose(1, 0, 2, 3, 4).reshape(CR, NBLK, BLK, BLK)

    return lax.map(row_tiles, jnp.arange(ROW_GRID, dtype=jnp.int32))
```

```python
import functools

import jax
import jax.numpy as jnp
from jax import lax
from jax.experimental import pallas as pl
from jax.experimental.pallas import tpu as pltpu
from jax.sharding import PartitionSpec as P

MESH = pl.DeviceIdType.MESH
BLK = 128
NCOL = 8
SLOTS = 3
NA = 16
NB = 6
HALF = NA // 2
AC = 4
AB = HALF // AC
BC = 2
BB = NB // BC
RX, RZ = 4, 8


def kernel(p_hbm, rows_s, targets_s, rows_v, out_ref, *scratch):
    a_bufs = scratch[0:4]
    tab_s = scratch[4:8]
    (b_buf, tab_v, bm_v, bm_s, p_v, ids, a_pick, b_pick, p_sem,
     a_recv, a_srecv, a_ssend, a_send, t_recv, t_send, t_sib,
     b_recv, b_send, m_recv, m_send, loc_sem, bm_sem) = scratch[8:]

    r, c = lax.axis_index("row"), lax.axis_index("col")
    x, y_lo = r % RX, r // RX
    core, z, y_hi = c % 2, (c // 2) % RZ, c // (2 * RZ)

    def device(x, y_lo, y_hi, z, core):
        return (y_lo * RX + x, (y_hi * RZ + z) * 2 + core)

    z_up = device(x, y_lo, y_hi, (z + 1) % RZ, core)
    z_down = device(x, y_lo, y_hi, (z + RZ - 1) % RZ, core)
    y_far = device(x, y_lo, 1 - y_hi, z, core)
    sib = device(x, y_lo, y_hi, z, 1 - core)
    x_up = device((x + 1) % RX, y_lo, y_hi, z, core)
    x_down = device((x + RX - 1) % RX, y_lo, y_hi, z, core)
    y_near = device(x, 1 - y_lo, y_hi, z, core)
    partners = (z_up, z_down, y_far, sib, x_up, x_down, y_near)

    barrier = pltpu.get_barrier_semaphore()
    for partner in partners:
        pl.semaphore_signal(barrier, inc=1, device_id=partner, device_id_type=MESH)

    a_root = (z % (RZ // 2) == 0) & (core == 0)
    b_root = x % (RX // 2) == 0
    fetch = pltpu.make_async_copy(p_hbm, p_v, p_sem)

    @pl.when(a_root | b_root)
    def _():
        fetch.start()
        ids[...] = jnp.full((8, 128), -1, jnp.int32)
        ids[0:SLOTS, 0:NCOL] = rows_v[...]

    for u in range(4):
        a_bufs[u][NA] = jnp.zeros((BLK, BLK), jnp.bfloat16)

    lane = lax.broadcasted_iota(jnp.int32, (8, 128), 1)
    sub = lax.broadcasted_iota(jnp.int32, (8, 128), 0)

    def running(stored):
        counts, total = [], jnp.int32(0)
        for e in range(SLOTS):
            for j in range(NCOL):
                total = total + stored(rows_s[e, j])
                counts.append(total)
        return counts

    def pick(counts, slots, out):
        for i in range(slots):
            place = jnp.int32(0)
            for count in counts[:-1]:
                place = place + jnp.where(count <= i, 1, 0)
            out[i] = place

    def prefix(ones):
        total = ones + pltpu.roll(ones, 1, 1)
        total = total + pltpu.roll(total, 2, 1)
        return total + pltpu.roll(total, 4, 1)

    @pl.when(b_root)
    def _():
        counts = running(lambda row: jnp.where((row >= 0) & (row < NCOL), 1, 0))
        pick(counts, NB, b_pick)
        held = ids[...]
        live = (held >= 0) & (held < NCOL)
        ones = jnp.where(live, 1, 0)
        base = jnp.where(sub == 1, counts[NCOL - 1], jnp.where(sub == 2, counts[2 * NCOL - 1], 0))
        v = x // (RX // 2)
        bm_v[v, 0] = jnp.where(live, held, NCOL)
        bm_v[v, 1] = jnp.where(live, jnp.minimum(prefix(ones) - ones + base, NB - 1), 0)

    @pl.when(a_root)
    def _():
        counts = running(lambda row: jnp.where(row >= 0, 1, 0))
        pick(counts, NA, a_pick)
        table = jnp.full((8, 128), NA, jnp.int32)
        wanted = (lane // 32) * 8 + sub
        for e in range(SLOTS):
            one = jnp.broadcast_to(ids[e:e + 1, :], (8, 128))
            two = jnp.maximum(one, pltpu.roll(one, 32, 1))
            four = jnp.maximum(two, pltpu.roll(two, 64, 1))
            ones = jnp.where(four >= 0, 1, 0)
            base = counts[e * NCOL - 1] if e else 0
            table = jnp.where(four == wanted, jnp.minimum(prefix(ones) - ones + base, NA), table)
        tab_v[z // (RZ // 2)] = table

    @pl.when(a_root | b_root)
    def _():
        fetch.wait()

    @pl.when(b_root)
    def _():
        for i in range(NB):
            b_buf[x // (RX // 2), i] = p_v[b_pick[i]]

    for v in range(2):
        @pl.when(a_root & (z == v * (RZ // 2)))
        def _(v=v):
            for i in range(NA):
                a_bufs[v][i] = p_v[a_pick[i]]

    pl.semaphore_wait(barrier, len(partners))

    def remote(src, dst, send, recv, to):
        return pltpu.make_async_remote_copy(
            src_ref=src, dst_ref=dst, send_sem=send, recv_sem=recv, device_id=to, device_id_type=MESH
        )

    def a_steps(u, k):
        flag, v = divmod(u, 2)
        d = (z + RZ - v * (RZ // 2)) % RZ
        first = k < AC // 2
        mine = pl.ds(core * HALF + k * AB, AB)
        other = pl.ds((1 - core) * HALF + k * AB, AB)
        part, far = a_bufs[u].at[mine], a_bufs[u].at[other]
        up = (d <= 3) if first else (d <= 2)
        down = (d == 0) | (d >= (6 if first else 5))
        out = []
        if flag == 0:
            root = (d == 0) & (core == 0)
            out.append((root, remote(far, far, a_ssend.at[u, AC + k], a_recv.at[u, k], sib)))
        out.append((up, remote(part, part, a_send.at[0, u, k], a_recv.at[u, k], z_up)))
        out.append((down, remote(part, part, a_send.at[1, u, k], a_recv.at[u, k], z_down)))
        if flag == 0:
            across = a_bufs[u + 2].at[mine]
            out.append((d == 0, remote(part, across, a_send.at[2, u, k], a_recv.at[u + 2, k], y_far)))
            beside = (d != 0) | (core == 0)
        else:
            beside = None
        out.append((beside, remote(part, part, a_ssend.at[u, k], a_srecv.at[u, k], sib)))
        return out

    def t_steps(u):
        flag, v = divmod(u, 2)
        d = (z + RZ - v * (RZ // 2)) % RZ
        part = tab_v.at[u]
        out = []
        if flag == 0:
            root = (d == 0) & (core == 0)
            out.append((root, remote(part, part, t_sib.at[u], t_recv.at[u], sib)))
        out.append((d <= 3, remote(part, part, t_send.at[0, u], t_recv.at[u], z_up)))
        out.append(((d == 0) | (d >= 6), remote(part, part, t_send.at[1, u], t_recv.at[u], z_down)))
        if flag == 0:
            out.append((d == 0, remote(part, tab_v.at[u + 2], t_send.at[2, u], t_recv.at[u + 2], y_far)))
        return out

    def b_steps(w, k):
        flag, v = divmod(w, 2)
        d = (x + RX - v * (RX // 2)) % RX
        if k is None:
            part, across = bm_v.at[w], bm_v.at[w % 2 + 2]
            send = lambda n: m_send.at[n, w]
            recv = lambda w: m_recv.at[w]
            up, down = d <= 1, d == 0
        else:
            part, across = b_buf.at[w, pl.ds(k * BB, BB)], b_buf.at[w % 2 + 2, pl.ds(k * BB, BB)]
            send = lambda n: b_send.at[n, w, k]
            recv = lambda w: b_recv.at[w, k]
            up = (d <= 1) if k < BC // 2 else (d == 0)
            down = (d == 0) if k < BC // 2 else ((d == 0) | (d == 3))
        out = [(up, remote(part, part, send(0), recv(w), x_up)), (down, remote(part, part, send(1), recv(w), x_down))]
        if flag == 0:
            out.append((d == 0, remote(part, across, send(2), recv(w + 2), y_near)))
        return out

    def start(steps):
        for condition, copy in steps:
            if condition is None:
                copy.start()
            else:
                pl.when(condition)(copy.start)

    def finish(steps):
        for condition, copy in steps:
            if condition is None:
                copy.wait_send()
            else:
                pl.when(condition)(copy.wait_send)

    def arrived(buf, sem):
        remote(buf, buf, loc_sem.at[0], sem, sib).wait_recv()

    def relay_a(u, k):
        flag, v = divmod(u, 2)
        mine = a_bufs[u].at[pl.ds(core * HALF + k * AB, AB)]
        if flag == 0:
            @pl.when((z != v * (RZ // 2)) | (core != 0))
            def _():
                arrived(mine, a_recv.at[u, k])
        else:
            arrived(mine, a_recv.at[u, k])
        start(a_steps(u, k))

    def relay_t(u):
        flag, v = divmod(u, 2)
        if flag == 0:
            @pl.when((z != v * (RZ // 2)) | (core != 0))
            def _():
                arrived(tab_v.at[u], t_recv.at[u])
        else:
            arrived(tab_v.at[u], t_recv.at[u])
        start(t_steps(u))
        pltpu.make_async_copy(tab_v.at[u], tab_s[u], loc_sem.at[u]).start()

    def relay_all(u):
        relay_t(u)
        for k in range(AC):
            relay_a(u, k)

    def b_wait(w):
        arrived(bm_v.at[w], m_recv.at[w])
        for k in range(BC):
            arrived(b_buf.at[w, pl.ds(k * BB, BB)], b_recv.at[w, k])

    def b_distance(w):
        return (x + RX - (w % 2) * (RX // 2)) % RX

    def relay_b(w, kind):
        d = b_distance(w)

        @pl.when((d == 0) if kind == "root" else (d % 2 == 1))
        def _():
            if kind == "root" and w < 2:
                start(b_steps(w, None))
                for k in range(BC):
                    start(b_steps(w, k))
            else:
                arrived(bm_v.at[w], m_recv.at[w])
                start(b_steps(w, None))
                for k in range(BC):
                    arrived(b_buf.at[w, pl.ds(k * BB, BB)], b_recv.at[w, k])
                    start(b_steps(w, k))

    for w in (0, 1):
        relay_b(w, "root")

    def b_first():
        for w in (2, 3):
            relay_b(w, "root")
        for w in (0, 1):
            relay_b(w, "odd")

    def b_second():
        for w in (2, 3):
            relay_b(w, "odd")

    for near in (0, 1):
        @pl.when((z % 4 != 2) & ((z + 2) // 4 % 2 == near))
        def _(near=near):
            relay_all(near)
            b_first()
            relay_all(near + 2)
            relay_all(1 - near)
            b_second()
            relay_all(3 - near)

    @pl.when(z % 4 == 2)
    def _():
        for pair in (0, 2):
            relay_t(pair)
            relay_t(pair + 1)
            for k in range(AC):
                relay_a(pair, k)
                relay_a(pair + 1, k)
            (b_second if pair else b_first)()

    for w in range(4):
        pl.when(b_distance(w) == 2)(functools.partial(b_wait, w))
    to_smem = pltpu.make_async_copy(bm_v, bm_s, bm_sem)
    to_smem.start()
    to_smem.wait()

    for u in range(4):
        flag, v = divmod(u, 2)
        pltpu.make_async_copy(tab_v.at[u], tab_s[u], loc_sem.at[u]).wait()
        other = lambda k: a_bufs[u].at[pl.ds((1 - core) * HALF + k * AB, AB)]
        for k in range(AC):
            if flag == 0:
                @pl.when((z != v * (RZ // 2)) | (core != 0))
                def _():
                    arrived(other(k), a_srecv.at[u, k])
            else:
                arrived(other(k), a_srecv.at[u, k])
        w = (flag + y_hi + y_lo) % 2 * 2 + v
        panel, table = a_bufs[u], tab_s[u]

        def column(j, _):
            places = []
            for s in range(SLOTS):
                target = targets_s[s, j]
                places.append((target % 8, target // 8 * 32))
            left, right = [], []
            for e in range(SLOTS):
                at = bm_s[w, 0, e, j]
                right.append(b_buf[w, bm_s[w, 1, e, j]])
                left.append(jnp.concatenate([panel[table[low, high + at]] for low, high in places], axis=0))
            term = jnp.dot(
                jnp.concatenate(left, axis=1), jnp.concatenate(right, axis=0), preferred_element_type=jnp.float32
            )
            for s in range(SLOTS):
                piece = term[s * BLK:(s + 1) * BLK]
                out_ref[s, j] = piece if u == 0 else out_ref[s, j] + piece
            return 0

        lax.fori_loop(0, NCOL, column, 0)

    for u in range(4):
        finish(t_steps(u))
        for k in range(AC):
            finish(a_steps(u, k))
    for w in range(4):
        finish(b_steps(w, None))
        for k in range(BC):
            finish(b_steps(w, k))


def local(p_blocks, p_rows, c_rows):
    blocks = p_blocks.reshape(SLOTS * NCOL, BLK, BLK)
    rows, targets = p_rows[0], c_rows[0]
    dma = pltpu.SemaphoreType.DMA
    out = pl.pallas_call(
        kernel,
        out_shape=jax.ShapeDtypeStruct((SLOTS, NCOL, BLK, BLK), jnp.float32),
        in_specs=[
            pl.BlockSpec(memory_space=pl.ANY),
            pl.BlockSpec(memory_space=pltpu.SMEM),
            pl.BlockSpec(memory_space=pltpu.SMEM),
            pl.BlockSpec(memory_space=pltpu.VMEM),
        ],
        out_specs=pl.BlockSpec(memory_space=pltpu.VMEM),
        scratch_shapes=[pltpu.VMEM((NA + 1, BLK, BLK), jnp.bfloat16)] * 4
        + [pltpu.SMEM((8, 128), jnp.int32)] * 4
        + [
            pltpu.VMEM((4, NB, BLK, BLK), jnp.bfloat16),
            pltpu.VMEM((4, 8, 128), jnp.int32),
            pltpu.VMEM((4, 2, 8, 128), jnp.int32),
            pltpu.SMEM((4, 2, 8, 128), jnp.int32),
            pltpu.VMEM((SLOTS * NCOL, BLK, BLK), jnp.bfloat16),
            pltpu.VMEM((8, 128), jnp.int32),
            pltpu.SMEM((NA,), jnp.int32),
            pltpu.SMEM((NB,), jnp.int32),
            dma,
            dma((4, AC)), dma((4, AC)), dma((4, 2 * AC)), dma((3, 4, AC)),
            dma((4,)), dma((3, 4)), dma((4,)),
            dma((4, BC)), dma((3, 4, BC)), dma((4,)), dma((3, 4)),
            dma((4,)), dma,
        ],
        compiler_params=pltpu.CompilerParams(
            collective_id=0, has_side_effects=True, vmem_limit_bytes=32 * 1024 * 1024
        ),
        name="panels",
    )(blocks, rows, targets, rows)
    return out[None]


def solution(mesh):
    placed = (P("row", None, "col", None, None), P("row", None, "col"), P("row", None, "col"))
    return jax.shard_map(
        local,
        mesh=mesh,
        in_specs=placed,
        out_specs=P("row", None, "col", None, None),
        check_vma=False,
    )
```

```python
import functools

import jax
import jax.numpy as jnp
from jax import lax
from jax.experimental import pallas as pl
from jax.experimental.pallas import tpu as pltpu
from jax.sharding import PartitionSpec as P

MESH = pl.DeviceIdType.MESH
BLK = 128
NCOL = 8
SLOTS = 3
NA = 16
NB = 6
HALF = NA // 2
AC = 8
AB = HALF // AC
EARLY = AC // 2
BC = 2
BB = NB // BC
RX, RZ = 4, 8


def kernel(p_hbm, rows_hbm, targets_hbm, out_hbm, *scratch):
    a_bufs = scratch[0:4]
    tab_s = scratch[4:8]
    (b_buf, tab_v, bm_v, bm_s, p_v, ids, a_pick, b_pick, p_sem,
     a_recv, a_srecv, a_ssend, a_send, t_recv, t_send, t_sib,
     b_recv, b_send, m_recv, m_send, loc_sem, bm_sem, rows_s, targets_s, rows_v, in_sem, acc, out_sem) = scratch[8:]

    r, c = lax.axis_index("row"), lax.axis_index("col")
    x, y_lo = r % RX, r // RX
    core, z, y_hi = c % 2, (c // 2) % RZ, c // (2 * RZ)

    def device(x, y_lo, y_hi, z, core):
        return (y_lo * RX + x, (y_hi * RZ + z) * 2 + core)

    z_up = device(x, y_lo, y_hi, (z + 1) % RZ, core)
    z_down = device(x, y_lo, y_hi, (z + RZ - 1) % RZ, core)
    y_far = device(x, y_lo, 1 - y_hi, z, core)
    sib = device(x, y_lo, y_hi, z, 1 - core)
    x_up = device((x + 1) % RX, y_lo, y_hi, z, core)
    x_down = device((x + RX - 1) % RX, y_lo, y_hi, z, core)
    y_near = device(x, 1 - y_lo, y_hi, z, core)
    partners = (z_up, z_down, y_far, sib, x_up, x_down, y_near)

    row_copy = pltpu.make_async_copy(rows_hbm, rows_s, in_sem.at[0])
    row_copy_v = pltpu.make_async_copy(rows_hbm, rows_v, in_sem.at[1])
    target_copy = pltpu.make_async_copy(targets_hbm, targets_s, in_sem.at[2])
    a_root = (z % (RZ // 2) == 0) & (core == 0)
    b_root = x % (RX // 2) == 0
    fetch = pltpu.make_async_copy(p_hbm, p_v, p_sem)

    @pl.when(a_root | b_root)
    def _():
        row_copy.start()
        row_copy_v.start()
        fetch.start()

    target_copy.start()

    barrier = pltpu.get_barrier_semaphore()
    for partner in partners:
        pl.semaphore_signal(barrier, inc=1, device_id=partner, device_id_type=MESH)

    @pl.when(a_root | b_root)
    def _():
        row_copy.wait()
        row_copy_v.wait()
        ids[...] = jnp.full((8, 128), -1, jnp.int32)
        for e in range(SLOTS):
            ids[e:e + 1, 0:NCOL] = rows_v[e]

    for u in range(4):
        a_bufs[u][NA] = jnp.zeros((BLK, BLK), jnp.bfloat16)

    lane = lax.broadcasted_iota(jnp.int32, (8, 128), 1)
    sub = lax.broadcasted_iota(jnp.int32, (8, 128), 0)

    def running(stored):
        counts, total = [], jnp.int32(0)
        for e in range(SLOTS):
            for j in range(NCOL):
                total = total + stored(rows_s[e, 0, j])
                counts.append(total)
        return counts

    def pick(counts, slots, out):
        for i in range(slots):
            place = jnp.int32(0)
            for count in counts[:-1]:
                place = place + jnp.where(count <= i, 1, 0)
            out[i] = place

    def prefix(ones):
        total = ones + pltpu.roll(ones, 1, 1)
        total = total + pltpu.roll(total, 2, 1)
        return total + pltpu.roll(total, 4, 1)

    @pl.when(b_root)
    def _():
        counts = running(lambda row: jnp.where((row >= 0) & (row < NCOL), 1, 0))
        pick(counts, NB, b_pick)
        held = ids[...]
        live = (held >= 0) & (held < NCOL)
        ones = jnp.where(live, 1, 0)
        base = jnp.where(sub == 1, counts[NCOL - 1], jnp.where(sub == 2, counts[2 * NCOL - 1], 0))
        v = x // (RX // 2)
        bm_v[v, 0] = jnp.where(live, held, NCOL)
        bm_v[v, 1] = jnp.where(live, jnp.minimum(prefix(ones) - ones + base, NB - 1), 0)

    @pl.when(a_root)
    def _():
        counts = running(lambda row: jnp.where(row >= 0, 1, 0))
        pick(counts, NA, a_pick)
        table = jnp.full((8, 128), NA, jnp.int32)
        wanted = (lane // 32) * 8 + sub
        for e in range(SLOTS):
            one = jnp.broadcast_to(ids[e:e + 1, :], (8, 128))
            two = jnp.maximum(one, pltpu.roll(one, 32, 1))
            four = jnp.maximum(two, pltpu.roll(two, 64, 1))
            ones = jnp.where(four >= 0, 1, 0)
            base = counts[e * NCOL - 1] if e else 0
            table = jnp.where(four == wanted, jnp.minimum(prefix(ones) - ones + base, NA), table)
        tab_v[z // (RZ // 2)] = table

    @pl.when(a_root | b_root)
    def _():
        fetch.wait()

    @pl.when(b_root)
    def _():
        for i in range(NB):
            b_buf[x // (RX // 2), i] = p_v[b_pick[i]]

    for v in range(2):
        @pl.when(a_root & (z == v * (RZ // 2)))
        def _(v=v):
            for i in range(NA):
                a_bufs[v][i] = p_v[a_pick[i]]

    pl.semaphore_wait(barrier, len(partners))

    def remote(src, dst, send, recv, to):
        return pltpu.make_async_remote_copy(
            src_ref=src, dst_ref=dst, send_sem=send, recv_sem=recv, device_id=to, device_id_type=MESH
        )

    def a_steps(u, k):
        flag, v = divmod(u, 2)
        d = (z + RZ - v * (RZ // 2)) % RZ
        mine = pl.ds(core * HALF + k * AB, AB)
        other = pl.ds((1 - core) * HALF + k * AB, AB)
        part, far = a_bufs[u].at[mine], a_bufs[u].at[other]
        even = k % 2 == 0
        up = (d <= 2) | ((d == 3) & even)
        down = (d == 0) | (d >= 6) | ((d == 5) & (k % 2 == 1))
        if flag:
            up, down = up & (k >= EARLY), down & (k >= EARLY)
        out = dict(
            up=(up, remote(part, part, a_send.at[0, u, k], a_recv.at[u, k], z_up)),
            down=(down, remote(part, part, a_send.at[1, u, k], a_recv.at[u, k], z_down)),
            side=(None, remote(part, part, a_ssend.at[u, k], a_srecv.at[u, k], sib)),
        )
        if flag == 0:
            across = a_bufs[u + 2].at[mine]
            out["side"] = ((d != 0) | (core == 0), out["side"][1])
            out["across"] = (
                (d == 0) | (k < EARLY), remote(part, across, a_send.at[2, u, k], a_recv.at[u + 2, k], y_far)
            )
            out["far"] = (
                (d == 0) & (core == 0), remote(far, far, a_ssend.at[u, AC + k], a_recv.at[u, k], sib)
            )
        return out

    def t_steps(u):
        flag, v = divmod(u, 2)
        d = (z + RZ - v * (RZ // 2)) % RZ
        part = tab_v.at[u]
        out = []
        if flag == 0:
            root = (d == 0) & (core == 0)
            out.append((root, remote(part, part, t_sib.at[u], t_recv.at[u], sib)))
        out.append((d <= 3, remote(part, part, t_send.at[0, u], t_recv.at[u], z_up)))
        out.append(((d == 0) | (d >= 6), remote(part, part, t_send.at[1, u], t_recv.at[u], z_down)))
        if flag == 0:
            out.append((d == 0, remote(part, tab_v.at[u + 2], t_send.at[2, u], t_recv.at[u + 2], y_far)))
        return out

    def b_steps(w, k):
        flag, v = divmod(w, 2)
        d = (x + RX - v * (RX // 2)) % RX
        if k is None:
            part, across = bm_v.at[w], bm_v.at[w % 2 + 2]
            send = lambda n: m_send.at[n, w]
            recv = lambda w: m_recv.at[w]
            up, down = d <= 1, d == 0
        else:
            part, across = b_buf.at[w, pl.ds(k * BB, BB)], b_buf.at[w % 2 + 2, pl.ds(k * BB, BB)]
            send = lambda n: b_send.at[n, w, k]
            recv = lambda w: b_recv.at[w, k]
            up = (d <= 1) if k < BC // 2 else (d == 0)
            down = (d == 0) if k < BC // 2 else ((d == 0) | (d == 3))
        out = [(up, remote(part, part, send(0), recv(w), x_up)), (down, remote(part, part, send(1), recv(w), x_down))]
        if flag == 0:
            out.append((d == 0, remote(part, across, send(2), recv(w + 2), y_near)))
        return out

    def start(steps):
        for condition, copy in steps:
            if condition is None:
                copy.start()
            else:
                pl.when(condition)(copy.start)

    def finish(steps):
        for condition, copy in steps:
            if condition is None:
                copy.wait_send()
            else:
                pl.when(condition)(copy.wait_send)

    def arrived(buf, sem):
        remote(buf, buf, loc_sem.at[0], sem, sib).wait_recv()

    def loop(body, low=0, high=AC):
        def step(k, _):
            body(k)
            return 0

        lax.fori_loop(low, high, step, 0)

    def mine(u, k):
        return a_bufs[u].at[pl.ds(core * HALF + k * AB, AB)]

    def relay_a(u, k):
        arrived(mine(u, k), a_recv.at[u, k])
        steps = a_steps(u, k)
        steps.pop("far", None)
        start(steps.values())

    def relay_own(u, between=None):
        root = z == u * (RZ // 2)

        @pl.when(z != u * (RZ // 2))
        def _():
            if between is None:
                loop(lambda k: relay_a(u, k))
            else:
                loop(lambda k: relay_a(u, k), 0, 3)
                between()
                loop(lambda k: relay_a(u, k), 3)

        @pl.when(root)
        def _():
            @pl.when(core == 0)
            def _():
                loop(lambda k: a_steps(u, k)["far"][1].start())

            @pl.when(core == 1)
            def _():
                loop(lambda k: arrived(mine(u, k), a_recv.at[u, k]))

            def send(k):
                steps = a_steps(u, k)
                steps["up"][1].start()
                steps["down"][1].start()
                a_steps(u, (k + EARLY) % AC)["across"][1].start()
                start([steps["side"]])

            loop(send)
            if between is not None:
                between()

    def relay_far(u, also=None, low=0, high=AC):
        def step(k):
            relay_a(u, (k + EARLY) % AC)
            if also is not None:
                also(k)

        loop(step, low, high)

    def send_out(j):
        return pltpu.make_async_copy(acc.at[:, j], out_hbm.at[:, j], out_sem.at[j])

    def relay_t(u):
        flag, v = divmod(u, 2)
        if flag == 0:
            @pl.when((z != v * (RZ // 2)) | (core != 0))
            def _():
                arrived(tab_v.at[u], t_recv.at[u])
        else:
            arrived(tab_v.at[u], t_recv.at[u])
        start(t_steps(u))
        pltpu.make_async_copy(tab_v.at[u], tab_s[u], loc_sem.at[u]).start()

    def b_wait(w):
        arrived(bm_v.at[w], m_recv.at[w])
        for k in range(BC):
            arrived(b_buf.at[w, pl.ds(k * BB, BB)], b_recv.at[w, k])

    def b_distance(w):
        return (x + RX - (w % 2) * (RX // 2)) % RX

    def relay_b(w, kind):
        d = b_distance(w)

        @pl.when((d == 0) if kind == "root" else (d % 2 == 1))
        def _():
            if kind == "root" and w < 2:
                start(b_steps(w, None))
                for k in range(BC):
                    start(b_steps(w, k))
            else:
                arrived(bm_v.at[w], m_recv.at[w])
                start(b_steps(w, None))
                for k in range(BC):
                    arrived(b_buf.at[w, pl.ds(k * BB, BB)], b_recv.at[w, k])
                    start(b_steps(w, k))

    for w in (0, 1):
        relay_b(w, "root")

    def b_first():
        for w in (2, 3):
            relay_b(w, "root")
        for w in (0, 1):
            relay_b(w, "odd")

    def b_second():
        for w in (2, 3):
            relay_b(w, "odd")

    def b_ready():
        for w in range(4):
            pl.when(b_distance(w) == 2)(functools.partial(b_wait, w))
        to_smem = pltpu.make_async_copy(bm_v, bm_s, bm_sem)
        to_smem.start()
        to_smem.wait()

    def a_ready(u):
        pltpu.make_async_copy(tab_v.at[u], tab_s[u], loc_sem.at[u]).wait()

        def wait(k):
            arrived(a_bufs[u].at[pl.ds((1 - core) * HALF + k * AB, AB)], a_srecv.at[u, k])

        if u < 2:
            @pl.when((z != u * (RZ // 2)) | (core != 0))
            def _():
                loop(wait)
        else:
            loop(wait)

    def column(u, j, first=False):
        flag, v = divmod(u, 2)
        w = (flag + y_hi + y_lo) % 2 * 2 + v
        panel, table = a_bufs[u], tab_s[u]
        places = []
        for s in range(SLOTS):
            target = targets_s[s, 0, j]
            places.append((target % 8, target // 8 * 32))
        left, right = [], []
        for e in range(SLOTS):
            at = bm_s[w, 0, e, j]
            right.append(b_buf[w, bm_s[w, 1, e, j]])
            left.append(jnp.concatenate([panel[table[low, high + at]] for low, high in places], axis=0))
        term = jnp.dot(
            jnp.concatenate(left, axis=1), jnp.concatenate(right, axis=0), preferred_element_type=jnp.float32
        )
        for s in range(SLOTS):
            piece = term[s * BLK:(s + 1) * BLK]
            acc[s, j] = piece if first else acc[s, j] + piece

    target_copy.wait()
    for near in (0, 1):
        @pl.when((z % 4 != 2) & ((z + 2) // 4 % 2 == near))
        def _(near=near):
            relay_t(near)
            relay_own(near, b_first)
            relay_t(near + 2)
            relay_far(near + 2, high=EARLY)
            b_second()
            relay_far(near + 2, low=EARLY)
            relay_t(1 - near)
            relay_own(1 - near)
            b_ready()
            relay_t(3 - near)
            for u in (near, near + 2, 1 - near):
                a_ready(u)

            def also(k):
                column(near, k, True)
                column(near + 2, k)
                column(1 - near, k)

            relay_far(3 - near, also)
            a_ready(3 - near)

            def last(j):
                column(3 - near, j)
                send_out(j).start()

            loop(last)

    @pl.when(z % 4 == 2)
    def _():
        b_first()
        for u in (0, 1):
            relay_t(u)

        def own(k):
            relay_a(0, k)
            relay_a(1, k)

        loop(own)
        b_second()
        for u in (2, 3):
            relay_t(u)

        def far(k):
            relay_a(2, (k + EARLY) % AC)
            relay_a(3, (k + EARLY) % AC)

        loop(far, 0, EARLY)
        b_ready()
        a_ready(0)
        a_ready(1)

        def far_and_columns(k):
            far(k)
            for part in range(2):
                j = (k - EARLY) * 2 + part
                column(0, j, True)
                column(1, j)

        loop(far_and_columns, EARLY)
        a_ready(2)
        a_ready(3)

        def last(j):
            column(2, j)
            column(3, j)
            send_out(j).start()

        loop(last)

    for u in range(4):
        finish(t_steps(u))
        loop(lambda k: finish(a_steps(u, k).values()))
    for w in range(4):
        finish(b_steps(w, None))
        for k in range(BC):
            finish(b_steps(w, k))
    loop(lambda j: send_out(j).wait())


def local(p_blocks, p_rows, c_rows):
    blocks = p_blocks.reshape(SLOTS * NCOL, BLK, BLK)
    rows, targets = p_rows.transpose(1, 0, 2), c_rows.transpose(1, 0, 2)
    dma = pltpu.SemaphoreType.DMA
    out = pl.pallas_call(
        kernel,
        out_shape=jax.ShapeDtypeStruct((SLOTS, NCOL, BLK, BLK), jnp.float32),
        in_specs=[
            pl.BlockSpec(memory_space=pl.ANY),
            pl.BlockSpec(memory_space=pl.ANY),
            pl.BlockSpec(memory_space=pl.ANY),
        ],
        out_specs=pl.BlockSpec(memory_space=pl.ANY),
        scratch_shapes=[pltpu.VMEM((NA + 1, BLK, BLK), jnp.bfloat16)] * 4
        + [pltpu.SMEM((8, 128), jnp.int32)] * 4
        + [
            pltpu.VMEM((4, NB, BLK, BLK), jnp.bfloat16),
            pltpu.VMEM((4, 8, 128), jnp.int32),
            pltpu.VMEM((4, 2, 8, 128), jnp.int32),
            pltpu.SMEM((4, 2, 8, 128), jnp.int32),
            pltpu.VMEM((SLOTS * NCOL, BLK, BLK), jnp.bfloat16),
            pltpu.VMEM((8, 128), jnp.int32),
            pltpu.SMEM((NA,), jnp.int32),
            pltpu.SMEM((NB,), jnp.int32),
            dma,
            dma((4, AC)), dma((4, AC)), dma((4, 2 * AC)), dma((3, 4, AC)),
            dma((4,)), dma((3, 4)), dma((4,)),
            dma((4, BC)), dma((3, 4, BC)), dma((4,)), dma((3, 4)),
            dma((4,)), dma,
            pltpu.SMEM((SLOTS, 1, NCOL), jnp.int32),
            pltpu.SMEM((SLOTS, 1, NCOL), jnp.int32),
            pltpu.VMEM((SLOTS, 1, NCOL), jnp.int32),
            dma((3,)),
            pltpu.VMEM((SLOTS, NCOL, BLK, BLK), jnp.float32),
            dma((NCOL,)),
        ],
        compiler_params=pltpu.CompilerParams(
            collective_id=0, has_side_effects=True, vmem_limit_bytes=60 * 1024 * 1024
        ),
        name="panels",
    )(blocks, rows, targets)
    return out[None]


def solution(mesh):
    placed = (P("row", None, "col", None, None), P("row", None, "col"), P("row", None, "col"))
    return jax.shard_map(
        local,
        mesh=mesh,
        in_specs=placed,
        out_specs=P("row", None, "col", None, None),
        check_vma=False,
    )
```

```python
import functools

import jax
import jax.numpy as jnp
from jax import lax
from jax.experimental import pallas as pl
from jax.experimental.pallas import tpu as pltpu
from jax.sharding import PartitionSpec as P

MESH = pl.DeviceIdType.MESH
BLK = 128
NCOL = 8
SLOTS = 3
NA = 16
NB = 6
HALF = NA // 2
AC = 8
AB = HALF // AC
EARLY = AC // 2
BC = 2
BB = NB // BC
RX, RZ = 4, 8


def kernel(p_hbm, rows_hbm, targets_hbm, acc, *scratch):
    a_bufs = scratch[0:4]
    tab_s = scratch[4:8]
    (b_buf, tab_v, bm_v, bm_s, p_v, ids, a_pick, b_pick, p_sem,
     a_recv, a_srecv, a_ssend, a_send, t_recv, t_send, t_sib,
     b_recv, b_send, m_recv, m_send, loc_sem, bm_sem, rows_s, targets_s, rows_v, in_sem, chain) = scratch[8:]

    r, c = lax.axis_index("row"), lax.axis_index("col")
    x, y_lo = r % RX, r // RX
    core, z, y_hi = c % 2, (c // 2) % RZ, c // (2 * RZ)

    def device(x, y_lo, y_hi, z, core):
        return (y_lo * RX + x, (y_hi * RZ + z) * 2 + core)

    z_up = device(x, y_lo, y_hi, (z + 1) % RZ, core)
    z_down = device(x, y_lo, y_hi, (z + RZ - 1) % RZ, core)
    y_far = device(x, y_lo, 1 - y_hi, z, core)
    sib = device(x, y_lo, y_hi, z, 1 - core)
    x_up = device((x + 1) % RX, y_lo, y_hi, z, core)
    x_down = device((x + RX - 1) % RX, y_lo, y_hi, z, core)
    x_far = device((x + RX // 2) % RX, y_lo, y_hi, z, core)
    y_near = device(x, 1 - y_lo, y_hi, z, core)
    partners = (z_up, z_down, y_far, sib, x_up, x_down, x_far, y_near)

    barrier = pltpu.get_barrier_semaphore()
    for partner in partners:
        pl.semaphore_signal(barrier, inc=1, device_id=partner, device_id_type=MESH)

    row_copy = pltpu.make_async_copy(rows_hbm, rows_s, in_sem.at[0])
    row_copy_v = pltpu.make_async_copy(rows_hbm, rows_v, in_sem.at[1])
    target_copy = pltpu.make_async_copy(targets_hbm, targets_s, in_sem.at[2])
    a_root = (z % (RZ // 2) == 0) & (core == 0)
    b_root = x % (RX // 2) == 0
    fetch = pltpu.make_async_copy(p_hbm, p_v, p_sem)

    @pl.when(a_root | b_root)
    def _():
        row_copy.start()
        row_copy_v.start()
        fetch.start()

    target_copy.start()

    for u in range(4):
        a_bufs[u][NA] = jnp.zeros((BLK, BLK), jnp.bfloat16)

    lane = lax.broadcasted_iota(jnp.int32, (8, 128), 1)
    sub = lax.broadcasted_iota(jnp.int32, (8, 128), 0)

    def pick(stored, slots, out):
        last = SLOTS * NCOL - 1
        here = jnp.int32(last)
        chain[last + 1] = here
        for f in range(last, -1, -1):
            here = jnp.where(stored(rows_s[f // NCOL, 0, f % NCOL]), f, here)
            chain[f] = here
        place = chain[0]
        out[0] = place
        for i in range(1, slots):
            place = chain[place + 1]
            out[i] = place

    def before(ones):
        return prefix(ones) - ones

    def row_sum(ones):
        return jnp.sum(ones, axis=1, keepdims=True)

    def prefix(ones):
        total = ones + pltpu.roll(ones, 1, 1)
        total = total + pltpu.roll(total, 2, 1)
        return total + pltpu.roll(total, 4, 1)

    def is_a(row):
        return row >= 0

    def is_b(row):
        return (row >= 0) & (row < NCOL)

    @pl.when(a_root | b_root)
    def _():
        row_copy.wait()

    @pl.when(a_root)
    def _():
        pick(is_a, NA, a_pick)

    @pl.when(b_root)
    def _():
        pick(is_b, NB, b_pick)

    def load_ids():
        row_copy_v.wait()
        ids[...] = jnp.full((8, 128), -1, jnp.int32)
        for e in range(SLOTS):
            ids[e:e + 1, 0:NCOL] = rows_v[e]

    def b_table():
        held = ids[...]
        live = is_b(held)
        ones = jnp.where(live, 1, 0)
        sums = row_sum(ones)
        base = jnp.where(sub >= 1, sums[0:1], 0) + jnp.where(sub >= 2, sums[1:2], 0)
        v = x // (RX // 2)
        bm_v[v, 0] = jnp.where(live, held, NCOL)
        bm_v[v, 1] = jnp.where(live, jnp.minimum(before(ones) + base, NB - 1), 0)

    def a_table():
        table = jnp.full((8, 128), NA, jnp.int32)
        wanted = lane // 32 * 8 + sub
        base = jnp.zeros((8, 1), jnp.int32)
        for e in range(SLOTS):
            one = jnp.broadcast_to(ids[e:e + 1, :], (8, 128))
            two = jnp.maximum(one, pltpu.roll(one, 32, 1))
            four = jnp.maximum(two, pltpu.roll(two, 64, 1))
            ones = jnp.where(is_a(four), 1, 0)
            table = jnp.where(four == wanted, jnp.minimum(before(ones) + base, NA), table)
            base = base + row_sum(ones) // 4
        tab_v[z // (RZ // 2)] = table

    @pl.when(a_root | b_root)
    def _():
        fetch.wait()

    @pl.when(b_root)
    def _():
        for i in range(NB):
            b_buf[x // (RX // 2), i] = p_v[b_pick[i]]

    for v in range(2):
        @pl.when(a_root & (z == v * (RZ // 2)))
        def _(v=v):
            for i in range(NA):
                a_bufs[v][i] = p_v[a_pick[i]]

    pl.semaphore_wait(barrier, len(partners))

    def remote(src, dst, send, recv, to):
        return pltpu.make_async_remote_copy(
            src_ref=src, dst_ref=dst, send_sem=send, recv_sem=recv, device_id=to, device_id_type=MESH
        )

    def a_steps(u, k):
        flag, v = divmod(u, 2)
        d = (z + RZ - v * (RZ // 2)) % RZ
        mine = pl.ds(core * HALF + k * AB, AB)
        other = pl.ds((1 - core) * HALF + k * AB, AB)
        part, far = a_bufs[u].at[mine], a_bufs[u].at[other]
        even = k % 2 == 0
        up = (d <= 2) | ((d == 3) & even)
        down = (d == 0) | (d >= 6) | ((d == 5) & (k % 2 == 1))
        if flag:
            up, down = up & (k >= EARLY), down & (k >= EARLY)
        out = dict(
            up=(up, remote(part, part, a_send.at[0, u, k], a_recv.at[u, k], z_up)),
            down=(down, remote(part, part, a_send.at[1, u, k], a_recv.at[u, k], z_down)),
            side=(None, remote(part, part, a_ssend.at[u, k], a_srecv.at[u, k], sib)),
        )
        if flag == 0:
            across = a_bufs[u + 2].at[mine]
            out["side"] = ((d != 0) | (core == 0), out["side"][1])
            out["across"] = (
                (d == 0) | (k < EARLY), remote(part, across, a_send.at[2, u, k], a_recv.at[u + 2, k], y_far)
            )
            out["far"] = (
                (d == 0) & (core == 0), remote(far, far, a_ssend.at[u, AC + k], a_recv.at[u, k], sib)
            )
        return out

    def t_steps(u):
        flag, v = divmod(u, 2)
        d = (z + RZ - v * (RZ // 2)) % RZ
        part = tab_v.at[u]
        out = []
        if flag == 0:
            root = (d == 0) & (core == 0)
            out.append((root, remote(part, part, t_sib.at[u], t_recv.at[u], sib)))
        out.append((d <= 3, remote(part, part, t_send.at[0, u], t_recv.at[u], z_up)))
        out.append(((d == 0) | (d >= 6), remote(part, part, t_send.at[1, u], t_recv.at[u], z_down)))
        if flag == 0:
            out.append((d == 0, remote(part, tab_v.at[u + 2], t_send.at[2, u], t_recv.at[u + 2], y_far)))
        return out

    def b_steps(w, k):
        flag, v = divmod(w, 2)
        d = (x + RX - v * (RX // 2)) % RX
        if k is None:
            part, across = bm_v.at[w], bm_v.at[w % 2 + 2]
            send = lambda n: m_send.at[n, w]
            recv = lambda w: m_recv.at[w]
        else:
            part, across = b_buf.at[w, pl.ds(k * BB, BB)], b_buf.at[w % 2 + 2, pl.ds(k * BB, BB)]
            send = lambda n: b_send.at[n, w, k]
            recv = lambda w: b_recv.at[w, k]
        out = []
        if flag == 0:
            out.append((d == 0, remote(part, across, send(3), recv(w + 2), y_near)))
        for n, to in enumerate((x_up, x_down, x_far)):
            out.append((d == 0, remote(part, part, send(n), recv(w), to)))
        return out

    def start(steps):
        for condition, copy in steps:
            if condition is None:
                copy.start()
            else:
                pl.when(condition)(copy.start)

    def finish(steps):
        for condition, copy in steps:
            if condition is None:
                copy.wait_send()
            else:
                pl.when(condition)(copy.wait_send)

    def arrived(buf, sem):
        remote(buf, buf, loc_sem.at[0], sem, sib).wait_recv()

    def loop(body, low=0, high=AC):
        def step(k, _):
            body(k)
            return 0

        lax.fori_loop(low, high, step, 0)

    def mine(u, k):
        return a_bufs[u].at[pl.ds(core * HALF + k * AB, AB)]

    def relay_a(u, k):
        arrived(mine(u, k), a_recv.at[u, k])
        steps = a_steps(u, k)
        steps.pop("far", None)
        start(steps.values())

    def order(i, side):
        base = i // 4 * 4 + i % 2 * 2 + i // 2 % 2
        return base + side * (1 - 2 * (base % 2))

    def side_of(u):
        return ((z + RZ - u % 2 * (RZ // 2)) % RZ + 3) // RZ

    def relay_range(u, low, high):
        side = side_of(u)
        loop(lambda i: relay_a(u, order(i, side)), low, high)

    def at_root(u):
        return z == u * (RZ // 2)

    def relay_own(u, between=None):
        @pl.when(~at_root(u))
        def _():
            if between is None:
                relay_range(u, 0, 6)
            else:
                relay_range(u, 0, 3)
                between()
                relay_range(u, 3, 6)

        @pl.when(at_root(u))
        def _():
            @pl.when(core == 0)
            def _():
                loop(lambda k: a_steps(u, k)["far"][1].start())

            @pl.when(core == 1)
            def _():
                loop(lambda k: arrived(mine(u, k), a_recv.at[u, k]))

            def send(i):
                a_steps(u, order(i, 0))["up"][1].start()
                a_steps(u, order(i, 1))["down"][1].start()

            def send_across(i):
                send(i)
                a_steps(u, order(i + EARLY, 0))["across"][1].start()

            loop(send_across, 0, EARLY)
            loop(send, EARLY, 6)
            loop(lambda k: start([a_steps(u, k)["side"]]))

    def relay_own_late(u):
        @pl.when(~at_root(u))
        def _():
            relay_range(u, 6, 8)

        @pl.when(at_root(u))
        def _():
            def send(i):
                a_steps(u, order(i, 0))["up"][1].start()
                a_steps(u, order(i, 1))["down"][1].start()

            loop(send, 6)
            loop(lambda i: a_steps(u, order(i, 0))["across"][1].start(), 0, EARLY)

    def relay_late(u):
        relay_range(u, EARLY, AC)

    def relay_early(u):
        relay_range(u, 0, EARLY)

    def relay_t(u):
        flag, v = divmod(u, 2)
        if flag == 0:
            @pl.when((z != v * (RZ // 2)) | (core != 0))
            def _():
                arrived(tab_v.at[u], t_recv.at[u])
        else:
            arrived(tab_v.at[u], t_recv.at[u])
        start(t_steps(u))
        pltpu.make_async_copy(tab_v.at[u], tab_s[u], loc_sem.at[u]).start()

    def b_wait(w):
        arrived(bm_v.at[w], m_recv.at[w])
        for k in range(BC):
            arrived(b_buf.at[w, pl.ds(k * BB, BB)], b_recv.at[w, k])

    def b_distance(w):
        return (x + RX - (w % 2) * (RX // 2)) % RX

    def send_b(w):
        @pl.when(b_distance(w) == 0)
        def _():
            for k in range(BC):
                if w >= 2:
                    arrived(b_buf.at[w, pl.ds(k * BB, BB)], b_recv.at[w, k])
                start(b_steps(w, k))
            if w >= 2:
                arrived(bm_v.at[w], m_recv.at[w])
                start(b_steps(w, None))

    for w in (0, 1):
        send_b(w)

    def b_own_tables():
        @pl.when(b_root)
        def _():
            b_table()
            for w in (0, 1):
                pl.when(b_distance(w) == 0)(lambda w=w: start(b_steps(w, None)))

    def b_peers():
        for w in (2, 3):
            send_b(w)

    def b_ready():
        for w in range(4):
            pl.when(b_distance(w) != 0)(functools.partial(b_wait, w))
        to_smem = pltpu.make_async_copy(bm_v, bm_s, bm_sem)
        to_smem.start()
        to_smem.wait()

    def a_ready(u):
        pltpu.make_async_copy(tab_v.at[u], tab_s[u], loc_sem.at[u]).wait()

        def wait(k):
            arrived(a_bufs[u].at[pl.ds((1 - core) * HALF + k * AB, AB)], a_srecv.at[u, k])

        if u < 2:
            @pl.when((z != u * (RZ // 2)) | (core != 0))
            def _():
                loop(wait)
        else:
            loop(wait)

    def column(pair, j, first):
        places = []
        for s in range(SLOTS):
            target = targets_s[s, 0, j]
            places.append((target % 8, target // 8 * 32))
        left, right = [], []
        for u in pair:
            flag, v = divmod(u, 2)
            w = (flag + y_hi + y_lo) % 2 * 2 + v
            panel, table = a_bufs[u], tab_s[u]
            for e in range(SLOTS):
                at = bm_s[w, 0, e, j]
                right.append(b_buf[w, bm_s[w, 1, e, j]])
                left.append([panel[table[low, high + at]] for low, high in places])
        right = jnp.concatenate(right, axis=0)
        for s in range(SLOTS):
            piece = jnp.dot(
                jnp.concatenate([blocks[s] for blocks in left], axis=1), right, preferred_element_type=jnp.float32
            )
            acc[s, j] = piece if first else acc[s, j] + piece

    target_copy.wait()
    def columns(pair, first):
        def step(i):
            for j in (i * 2, i * 2 + 1):
                column(pair, j, first)

        loop(step, 0, NCOL // 2)

    for near in (0, 1):
        @pl.when((z % 4 != 2) & ((z + 2) // 4 % 2 == near))
        def _(near=near):
            far = 1 - near
            relay_own(near)
            pl.when(a_root | b_root)(load_ids)
            pl.when(a_root)(a_table)
            relay_t(near)
            b_own_tables()
            pl.when(z % 4 != 0)(b_peers)
            relay_late(near + 2)
            relay_t(near + 2)
            relay_own_late(near)
            pl.when(z % 4 == 0)(b_peers)
            relay_early(near + 2)
            relay_own(far)
            relay_t(far)

            @pl.when(z % 4 == 0)
            def _():
                relay_own_late(far)

            @pl.when(z % 4 != 0)
            def _():
                relay_late(far + 2)
                relay_t(far + 2)

            b_ready()
            a_ready(near)
            a_ready(near + 2)

            @pl.when(z % 4 == 0)
            def _():
                def step(i):
                    column((near, near + 2), i * 2, True)
                    column((near, near + 2), i * 2 + 1, True)
                    relay_a(far + 2, order(i + EARLY, side_of(far)))

                loop(step, 0, EARLY)
                relay_t(far + 2)
                relay_early(far + 2)

            @pl.when(z % 4 != 0)
            def _():
                def step(i):
                    relay_a(far + 2, order(i, side_of(far)))

                    @pl.when(i >= 2)
                    def _():
                        relay_a(far, order(i + EARLY, side_of(far)))

                    column((near, near + 2), i * 2, True)
                    column((near, near + 2), i * 2 + 1, True)

                loop(step, 0, EARLY)

            a_ready(far)
            a_ready(far + 2)

            columns((far, far + 2), False)

    @pl.when(z % 4 == 2)
    def _():
        @pl.when(b_root)
        def _():
            load_ids()

        b_own_tables()

        def both(u, low, high):
            def step(i):
                relay_a(u, order(i, side_of(0)))
                relay_a(u + 1, order(i, side_of(1)))

            loop(step, low, high)

        both(0, 0, 3)
        b_peers()
        both(0, 3, 6)
        relay_t(0)
        relay_t(1)
        both(2, EARLY, AC)
        relay_t(2)
        relay_t(3)
        both(0, 6, AC)
        both(2, 0, EARLY)
        b_ready()
        a_ready(0)
        a_ready(2)
        columns((0, 2), True)
        a_ready(1)
        a_ready(3)

        columns((1, 3), False)

    for u in range(4):
        finish(t_steps(u))
        loop(lambda k: finish(a_steps(u, k).values()))
    for w in range(4):
        finish(b_steps(w, None))
        for k in range(BC):
            finish(b_steps(w, k))


def local(p_blocks, p_rows, c_rows):
    blocks = p_blocks.reshape(SLOTS * NCOL, BLK, BLK)
    rows, targets = p_rows.transpose(1, 0, 2), c_rows.transpose(1, 0, 2)
    dma = pltpu.SemaphoreType.DMA
    out = pl.pallas_call(
        kernel,
        out_shape=pltpu.VMEM((SLOTS, NCOL, BLK, BLK), jnp.float32),
        in_specs=[
            pl.BlockSpec(memory_space=pl.ANY),
            pl.BlockSpec(memory_space=pl.ANY),
            pl.BlockSpec(memory_space=pl.ANY),
        ],
        out_specs=pl.BlockSpec(memory_space=pltpu.VMEM),
        scratch_shapes=[pltpu.VMEM((NA + 1, BLK, BLK), jnp.bfloat16)] * 4
        + [pltpu.SMEM((8, 128), jnp.int32)] * 4
        + [
            pltpu.VMEM((4, NB, BLK, BLK), jnp.bfloat16),
            pltpu.VMEM((4, 8, 128), jnp.int32),
            pltpu.VMEM((4, 2, 8, 128), jnp.int32),
            pltpu.SMEM((4, 2, 8, 128), jnp.int32),
            pltpu.VMEM((SLOTS * NCOL, BLK, BLK), jnp.bfloat16),
            pltpu.VMEM((8, 128), jnp.int32),
            pltpu.SMEM((NA,), jnp.int32),
            pltpu.SMEM((NB,), jnp.int32),
            dma,
            dma((4, AC)), dma((4, AC)), dma((4, 2 * AC)), dma((3, 4, AC)),
            dma((4,)), dma((3, 4)), dma((4,)),
            dma((4, BC)), dma((4, 4, BC)), dma((4,)), dma((4, 4)),
            dma((4,)), dma,
            pltpu.SMEM((SLOTS, 1, NCOL), jnp.int32),
            pltpu.SMEM((SLOTS, 1, NCOL), jnp.int32),
            pltpu.VMEM((SLOTS, 1, NCOL), jnp.int32),
            dma((3,)),
            pltpu.SMEM((SLOTS * NCOL + 1,), jnp.int32),
        ],
        compiler_params=pltpu.CompilerParams(
            collective_id=0, has_side_effects=True, vmem_limit_bytes=(65536 - 4096) * 1024
        ),
        name="panels",
    )(blocks, rows, targets)
    return out[None]


def solution(mesh):
    placed = (P("row", None, "col", None, None), P("row", None, "col"), P("row", None, "col"))
    return jax.shard_map(
        local,
        mesh=mesh,
        in_specs=placed,
        out_specs=P("row", None, "col", None, None),
        check_vma=False,
    )
```

```python
import functools

import jax
import jax.numpy as jnp
from jax import lax
from jax.experimental import pallas as pl
from jax.experimental.pallas import tpu as pltpu
from jax.sharding import PartitionSpec as P

MESH = pl.DeviceIdType.MESH
BLK = 128
NCOL = 8
SLOTS = 3
NA = 16
NB = 6
HALF = NA // 2
AC = 8
AB = HALF // AC
EARLY = AC // 2
BC = 2
BB = NB // BC
RX, RZ = 4, 8


def kernel(p_hbm, rows_hbm, targets_hbm, acc, *scratch):
    a_bufs = scratch[0:4]
    tab_s = scratch[4:8]
    (b_buf, tab_v, bm_v, bm_s, p_v, ids, a_pick, b_pick, p_sem,
     a_recv, a_srecv, a_ssend, a_send, t_recv, t_send, t_sib,
     b_recv, b_send, m_recv, m_send, loc_sem, bm_sem, rows_s, targets_s, rows_v, in_sem, chain) = scratch[8:]

    r, c = lax.axis_index("row"), lax.axis_index("col")
    x, y_lo = r % RX, r // RX
    core, z, y_hi = c % 2, (c // 2) % RZ, c // (2 * RZ)

    def device(x, y_lo, y_hi, z, core):
        return (y_lo * RX + x, (y_hi * RZ + z) * 2 + core)

    z_up = device(x, y_lo, y_hi, (z + 1) % RZ, core)
    z_down = device(x, y_lo, y_hi, (z + RZ - 1) % RZ, core)
    y_far = device(x, y_lo, 1 - y_hi, z, core)
    sib = device(x, y_lo, y_hi, z, 1 - core)
    x_up = device((x + 1) % RX, y_lo, y_hi, z, core)
    x_down = device((x + RX - 1) % RX, y_lo, y_hi, z, core)
    x_far = device((x + RX // 2) % RX, y_lo, y_hi, z, core)
    y_near = device(x, 1 - y_lo, y_hi, z, core)
    partners = (z_up, z_down, y_far, sib, x_up, x_down, x_far, y_near)

    barrier = pltpu.get_barrier_semaphore()
    for partner in partners:
        pl.semaphore_signal(barrier, inc=1, device_id=partner, device_id_type=MESH)

    row_copy = pltpu.make_async_copy(rows_hbm, rows_s, in_sem.at[0])
    row_copy_v = pltpu.make_async_copy(rows_hbm, rows_v, in_sem.at[1])
    target_copy = pltpu.make_async_copy(targets_hbm, targets_s, in_sem.at[2])
    a_root = (z % (RZ // 2) == 0) & (core == 0)
    b_root = x % (RX // 2) == 0
    fetch = pltpu.make_async_copy(p_hbm, p_v, p_sem)

    @pl.when(a_root | b_root)
    def _():
        row_copy.start()
        row_copy_v.start()
        fetch.start()

    target_copy.start()

    for u in range(4):
        a_bufs[u][NA] = jnp.zeros((BLK, BLK), jnp.bfloat16)

    lane = lax.broadcasted_iota(jnp.int32, (8, 128), 1)
    sub = lax.broadcasted_iota(jnp.int32, (8, 128), 0)

    def pick(stored, slots, out):
        last = SLOTS * NCOL - 1
        here = jnp.int32(last)
        chain[last + 1] = here
        for f in range(last, -1, -1):
            here = jnp.where(stored(rows_s[f // NCOL, 0, f % NCOL]), f, here)
            chain[f] = here
        place = chain[0]
        out[0] = place
        for i in range(1, slots):
            place = chain[place + 1]
            out[i] = place

    def before(ones):
        return prefix(ones) - ones

    def row_sum(ones):
        return jnp.sum(ones, axis=1, keepdims=True)

    def prefix(ones):
        total = ones + pltpu.roll(ones, 1, 1)
        total = total + pltpu.roll(total, 2, 1)
        return total + pltpu.roll(total, 4, 1)

    def is_a(row):
        return row >= 0

    def is_b(row):
        return (row >= 0) & (row < NCOL)

    @pl.when(a_root | b_root)
    def _():
        row_copy.wait()

    @pl.when(a_root)
    def _():
        pick(is_a, NA, a_pick)

    def load_ids():
        row_copy_v.wait()
        ids[...] = jnp.full((8, 128), -1, jnp.int32)
        for e in range(SLOTS):
            ids[e:e + 1, 0:NCOL] = rows_v[e]

    def b_table():
        held = ids[...]
        live = is_b(held)
        ones = jnp.where(live, 1, 0)
        sums = row_sum(ones)
        base = jnp.where(sub >= 1, sums[0:1], 0) + jnp.where(sub >= 2, sums[1:2], 0)
        v = x // (RX // 2)
        bm_v[v, 0] = jnp.where(live, held, NCOL)
        bm_v[v, 1] = jnp.where(live, jnp.minimum(before(ones) + base, NB - 1), 0)

    def a_table():
        table = jnp.full((8, 128), NA, jnp.int32)
        wanted = lane // 32 * 8 + sub
        base = jnp.zeros((8, 1), jnp.int32)
        for e in range(SLOTS):
            one = jnp.broadcast_to(ids[e:e + 1, :], (8, 128))
            two = jnp.maximum(one, pltpu.roll(one, 32, 1))
            four = jnp.maximum(two, pltpu.roll(two, 64, 1))
            ones = jnp.where(is_a(four), 1, 0)
            table = jnp.where(four == wanted, jnp.minimum(before(ones) + base, NA), table)
            base = base + row_sum(ones) // 4
        tab_v[z // (RZ // 2)] = table

    @pl.when(a_root | b_root)
    def _():
        fetch.wait()

    for v in range(2):
        @pl.when(a_root & (z == v * (RZ // 2)))
        def _(v=v):
            for i in range(NA):
                a_bufs[v][i] = p_v[a_pick[i]]

    pl.semaphore_wait(barrier, len(partners))

    def remote(src, dst, send, recv, to):
        return pltpu.make_async_remote_copy(
            src_ref=src, dst_ref=dst, send_sem=send, recv_sem=recv, device_id=to, device_id_type=MESH
        )

    def a_steps(u, k):
        flag, v = divmod(u, 2)
        d = (z + RZ - v * (RZ // 2)) % RZ
        mine = pl.ds(core * HALF + k * AB, AB)
        other = pl.ds((1 - core) * HALF + k * AB, AB)
        part, far = a_bufs[u].at[mine], a_bufs[u].at[other]
        even = k % 2 == 0
        up = (d <= 2) | ((d == 3) & even)
        down = (d == 0) | (d >= 6) | ((d == 5) & (k % 2 == 1))
        if flag:
            up, down = up & (k >= EARLY), down & (k >= EARLY)
        out = dict(
            up=(up, remote(part, part, a_send.at[0, u, k], a_recv.at[u, k], z_up)),
            down=(down, remote(part, part, a_send.at[1, u, k], a_recv.at[u, k], z_down)),
            side=(None, remote(part, part, a_ssend.at[u, k], a_srecv.at[u, k], sib)),
        )
        if flag == 0:
            across = a_bufs[u + 2].at[mine]
            out["side"] = ((d != 0) | (core == 0), out["side"][1])
            out["across"] = (
                (d == 0) | (k < EARLY), remote(part, across, a_send.at[2, u, k], a_recv.at[u + 2, k], y_far)
            )
            out["far"] = (
                (d == 0) & (core == 0), remote(far, far, a_ssend.at[u, AC + k], a_recv.at[u, k], sib)
            )
        return out

    def t_steps(u):
        flag, v = divmod(u, 2)
        d = (z + RZ - v * (RZ // 2)) % RZ
        part = tab_v.at[u]
        out = []
        if flag == 0:
            root = (d == 0) & (core == 0)
            out.append((root, remote(part, part, t_sib.at[u], t_recv.at[u], sib)))
        out.append((d <= 3, remote(part, part, t_send.at[0, u], t_recv.at[u], z_up)))
        out.append(((d == 0) | (d >= 6), remote(part, part, t_send.at[1, u], t_recv.at[u], z_down)))
        if flag == 0:
            out.append((d == 0, remote(part, tab_v.at[u + 2], t_send.at[2, u], t_recv.at[u + 2], y_far)))
        return out

    def b_steps(w, k):
        flag, v = divmod(w, 2)
        d = (x + RX - v * (RX // 2)) % RX
        if k is None:
            part, across = bm_v.at[w], bm_v.at[w % 2 + 2]
            send = lambda n: m_send.at[n, w]
            recv = lambda w: m_recv.at[w]
        else:
            part, across = b_buf.at[w, pl.ds(k * BB, BB)], b_buf.at[w % 2 + 2, pl.ds(k * BB, BB)]
            send = lambda n: b_send.at[n, w, k]
            recv = lambda w: b_recv.at[w, k]
        out = []
        if flag == 0:
            out.append((d != 2 if k == 0 else d == 0, remote(part, across, send(3), recv(w + 2), y_near)))
        for n, to in enumerate((x_up, x_down, x_far)):
            if n == 2 or flag == 0 or k != 0:
                out.append((d == 0, remote(part, part, send(n), recv(w), to)))
        return out

    def start(steps):
        for condition, copy in steps:
            if condition is None:
                copy.start()
            else:
                pl.when(condition)(copy.start)

    def finish(steps):
        for condition, copy in steps:
            if condition is None:
                copy.wait_send()
            else:
                pl.when(condition)(copy.wait_send)

    def arrived(buf, sem):
        remote(buf, buf, loc_sem.at[0], sem, sib).wait_recv()

    def loop(body, low=0, high=AC):
        def step(k, _):
            body(k)
            return 0

        lax.fori_loop(low, high, step, 0)

    def mine(u, k):
        return a_bufs[u].at[pl.ds(core * HALF + k * AB, AB)]

    def relay_a(u, k):
        arrived(mine(u, k), a_recv.at[u, k])
        steps = a_steps(u, k)
        steps.pop("far", None)
        start(steps.values())

    def order(i, side):
        base = i // 4 * 4 + i % 2 * 2 + i // 2 % 2
        return base + side * (1 - 2 * (base % 2))

    def side_of(u):
        return ((z + RZ - u % 2 * (RZ // 2)) % RZ + 3) // RZ

    def relay_range(u, low, high):
        side = side_of(u)
        loop(lambda i: relay_a(u, order(i, side)), low, high)

    def at_root(u):
        return z == u * (RZ // 2)

    def relay_own(u, between=None):
        @pl.when(~at_root(u))
        def _():
            if between is None:
                relay_range(u, 0, 6)
            else:
                relay_range(u, 0, 3)
                between()
                relay_range(u, 3, 6)

        @pl.when(at_root(u))
        def _():
            @pl.when(core == 0)
            def _():
                loop(lambda k: a_steps(u, k)["far"][1].start())

            @pl.when(core == 1)
            def _():
                loop(lambda k: arrived(mine(u, k), a_recv.at[u, k]))

            def send(i):
                a_steps(u, order(i, 0))["up"][1].start()
                a_steps(u, order(i, 1))["down"][1].start()

            def send_across(i):
                send(i)
                a_steps(u, order(i + EARLY, 0))["across"][1].start()

            loop(send_across, 0, EARLY)
            loop(send, EARLY, 6)
            loop(lambda k: start([a_steps(u, k)["side"]]))

    def relay_own_late(u):
        @pl.when(~at_root(u))
        def _():
            relay_range(u, 6, 8)

        @pl.when(at_root(u))
        def _():
            def send(i):
                a_steps(u, order(i, 0))["up"][1].start()
                a_steps(u, order(i, 1))["down"][1].start()

            loop(send, 6)
            loop(lambda i: a_steps(u, order(i, 0))["across"][1].start(), 0, EARLY)

    def relay_late(u):
        relay_range(u, EARLY, AC)

    def relay_early(u):
        relay_range(u, 0, EARLY)

    def relay_t(u):
        flag, v = divmod(u, 2)
        if flag == 0:
            @pl.when((z != v * (RZ // 2)) | (core != 0))
            def _():
                arrived(tab_v.at[u], t_recv.at[u])
        else:
            arrived(tab_v.at[u], t_recv.at[u])
        start(t_steps(u))
        pltpu.make_async_copy(tab_v.at[u], tab_s[u], loc_sem.at[u]).start()

    def b_wait(w):
        arrived(bm_v.at[w], m_recv.at[w])
        for k in range(BC):
            def wait(k=k):
                arrived(b_buf.at[w, pl.ds(k * BB, BB)], b_recv.at[w, k])

            if w < 2 and k == 0:
                pl.when(b_distance(w) == 2)(wait)
            else:
                wait()

    def b_distance(w):
        return (x + RX - (w % 2) * (RX // 2)) % RX

    def send_b(w):
        @pl.when(b_distance(w) == 0)
        def _():
            for k in range(BC):
                if w >= 2:
                    arrived(b_buf.at[w, pl.ds(k * BB, BB)], b_recv.at[w, k])
                start(b_steps(w, k)[:-1])
            for k in range(BC):
                start(b_steps(w, k)[-1:])
            if w >= 2:
                arrived(bm_v.at[w], m_recv.at[w])
                start(b_steps(w, None))

    def b_begin():
        @pl.when(b_root)
        def _():
            pick(is_b, NB, b_pick)
            for i in range(NB):
                b_buf[x // (RX // 2), i] = p_v[b_pick[i]]

        for w in (0, 1):
            send_b(w)

    pl.when(~a_root)(b_begin)

    def b_own_tables():
        @pl.when(b_root)
        def _():
            b_table()
            for w in (0, 1):
                pl.when(b_distance(w) == 0)(lambda w=w: start(b_steps(w, None)))

    def b_peers():
        for w in (0, 1):
            @pl.when(b_distance(w) % 2 == 1)
            def _(w=w):
                arrived(b_buf.at[w, pl.ds(0, BB)], b_recv.at[w, 0])
                start(b_steps(w, 0)[:1])

        for w in (2, 3):
            send_b(w)

    def b_ready():
        for w in range(4):
            pl.when(b_distance(w) != 0)(functools.partial(b_wait, w))
        to_smem = pltpu.make_async_copy(bm_v, bm_s, bm_sem)
        to_smem.start()
        to_smem.wait()

    def a_ready(u):
        pltpu.make_async_copy(tab_v.at[u], tab_s[u], loc_sem.at[u]).wait()

        def wait(k):
            arrived(a_bufs[u].at[pl.ds((1 - core) * HALF + k * AB, AB)], a_srecv.at[u, k])

        if u < 2:
            @pl.when((z != u * (RZ // 2)) | (core != 0))
            def _():
                loop(wait)
        else:
            loop(wait)

    def column(pair, j, first):
        places = []
        for s in range(SLOTS):
            target = targets_s[s, 0, j]
            places.append((target % 8, target // 8 * 32))
        left, right = [], []
        for u in pair:
            flag, v = divmod(u, 2)
            w = (flag + y_hi + y_lo) % 2 * 2 + v
            panel, table = a_bufs[u], tab_s[u]
            for e in range(SLOTS):
                at = bm_s[w, 0, e, j]
                right.append(b_buf[w, bm_s[w, 1, e, j]])
                left.append([panel[table[low, high + at]] for low, high in places])
        right = jnp.concatenate(right, axis=0)
        for s in range(SLOTS):
            piece = jnp.dot(
                jnp.concatenate([blocks[s] for blocks in left], axis=1), right, preferred_element_type=jnp.float32
            )
            acc[s, j] = piece if first else acc[s, j] + piece

    target_copy.wait()
    def columns(pair, first):
        def step(i):
            for j in (i * 2, i * 2 + 1):
                column(pair, j, first)

        loop(step, 0, NCOL // 2)

    for near in (0, 1):
        @pl.when((z % 4 != 2) & ((z + 2) // 4 % 2 == near))
        def _(near=near):
            far = 1 - near
            relay_own(near)
            pl.when(a_root)(b_begin)
            pl.when(a_root | b_root)(load_ids)
            pl.when(a_root)(a_table)
            relay_t(near)
            b_own_tables()
            pl.when(z % 4 != 0)(b_peers)
            relay_late(near + 2)
            relay_t(near + 2)
            relay_own_late(near)
            pl.when(z % 4 == 0)(b_peers)
            relay_early(near + 2)
            relay_own(far)
            relay_t(far)

            @pl.when(z % 4 == 0)
            def _():
                relay_own_late(far)

            @pl.when(z % 4 != 0)
            def _():
                relay_late(far + 2)
                relay_t(far + 2)

            b_ready()
            a_ready(near)
            a_ready(near + 2)

            @pl.when(z % 4 == 0)
            def _():
                def step(i):
                    column((near, near + 2), i * 2, True)
                    column((near, near + 2), i * 2 + 1, True)
                    relay_a(far + 2, order(i + EARLY, side_of(far)))

                loop(step, 0, EARLY)
                relay_t(far + 2)
                relay_early(far + 2)

            @pl.when(z % 4 != 0)
            def _():
                def step(i):
                    relay_a(far + 2, order(i, side_of(far)))

                    @pl.when(i >= 2)
                    def _():
                        relay_a(far, order(i + EARLY, side_of(far)))

                    column((near, near + 2), i * 2, True)
                    column((near, near + 2), i * 2 + 1, True)

                loop(step, 0, EARLY)

            a_ready(far)
            a_ready(far + 2)

            columns((far, far + 2), False)

    @pl.when(z % 4 == 2)
    def _():
        @pl.when(b_root)
        def _():
            load_ids()

        b_own_tables()

        def both(u, low, high):
            def step(i):
                relay_a(u, order(i, side_of(0)))
                relay_a(u + 1, order(i, side_of(1)))

            loop(step, low, high)

        both(0, 0, 3)
        b_peers()
        both(0, 3, 6)
        relay_t(0)
        relay_t(1)
        both(2, EARLY, AC)
        relay_t(2)
        relay_t(3)
        both(0, 6, AC)
        both(2, 0, EARLY)
        b_ready()
        a_ready(0)
        a_ready(2)
        columns((0, 2), True)
        a_ready(1)
        a_ready(3)

        columns((1, 3), False)

    for u in range(4):
        finish(t_steps(u))
        loop(lambda k: finish(a_steps(u, k).values()))
    for w in range(4):
        finish(b_steps(w, None))
        for k in range(BC):
            finish(b_steps(w, k))


def local(p_blocks, p_rows, c_rows):
    blocks = p_blocks.reshape(SLOTS * NCOL, BLK, BLK)
    rows, targets = p_rows.transpose(1, 0, 2), c_rows.transpose(1, 0, 2)
    dma = pltpu.SemaphoreType.DMA
    out = pl.pallas_call(
        kernel,
        out_shape=pltpu.VMEM((SLOTS, NCOL, BLK, BLK), jnp.float32),
        in_specs=[
            pl.BlockSpec(memory_space=pl.ANY),
            pl.BlockSpec(memory_space=pl.ANY),
            pl.BlockSpec(memory_space=pl.ANY),
        ],
        out_specs=pl.BlockSpec(memory_space=pltpu.VMEM),
        scratch_shapes=[pltpu.VMEM((NA + 1, BLK, BLK), jnp.bfloat16)] * 4
        + [pltpu.SMEM((8, 128), jnp.int32)] * 4
        + [
            pltpu.VMEM((4, NB, BLK, BLK), jnp.bfloat16),
            pltpu.VMEM((4, 8, 128), jnp.int32),
            pltpu.VMEM((4, 2, 8, 128), jnp.int32),
            pltpu.SMEM((4, 2, 8, 128), jnp.int32),
            pltpu.VMEM((SLOTS * NCOL, BLK, BLK), jnp.bfloat16),
            pltpu.VMEM((8, 128), jnp.int32),
            pltpu.SMEM((NA,), jnp.int32),
            pltpu.SMEM((NB,), jnp.int32),
            dma,
            dma((4, AC)), dma((4, AC)), dma((4, 2 * AC)), dma((3, 4, AC)),
            dma((4,)), dma((3, 4)), dma((4,)),
            dma((4, BC)), dma((4, 4, BC)), dma((4,)), dma((4, 4)),
            dma((4,)), dma,
            pltpu.SMEM((SLOTS, 1, NCOL), jnp.int32),
            pltpu.SMEM((SLOTS, 1, NCOL), jnp.int32),
            pltpu.VMEM((SLOTS, 1, NCOL), jnp.int32),
            dma((3,)),
            pltpu.SMEM((SLOTS * NCOL + 1,), jnp.int32),
        ],
        compiler_params=pltpu.CompilerParams(
            collective_id=0, has_side_effects=True, vmem_limit_bytes=(65536 - 4096) * 1024
        ),
        name="panels",
    )(blocks, rows, targets)
    return out[None]


def solution(mesh):
    placed = (P("row", None, "col", None, None), P("row", None, "col"), P("row", None, "col"))
    return jax.shard_map(
        local,
        mesh=mesh,
        in_specs=placed,
        out_specs=P("row", None, "col", None, None),
        check_vma=False,
    )
```

```python
import functools

import jax
import jax.numpy as jnp
from jax import lax
from jax.experimental import pallas as pl
from jax.experimental.pallas import tpu as pltpu
from jax.sharding import PartitionSpec as P

MESH = pl.DeviceIdType.MESH
BLK = 128
NCOL = 8
SLOTS = 3
NA = 16
NB = 6
HALF = NA // 2
AC = 8
AB = HALF // AC
EARLY = AC // 2
BC = 2
BB = NB // BC
RX, RZ = 4, 8


def kernel(p_hbm, rows_hbm, targets_hbm, acc, *scratch):
    a_bufs = scratch[0:4]
    tab_s = scratch[4:8]
    (b_buf, tab_v, bm_v, bm_s, p_v, ids, a_pick, b_pick, p_sem,
     a_recv, a_srecv, a_ssend, a_send, t_recv, t_send, t_sib,
     b_recv, b_send, m_recv, m_send, loc_sem, bm_sem, rows_s, targets_s, rows_v, in_sem, chain) = scratch[8:]

    r, c = lax.axis_index("row"), lax.axis_index("col")
    x, y_lo = r % RX, r // RX
    core, z, y_hi = c % 2, (c // 2) % RZ, c // (2 * RZ)

    def device(x, y_lo, y_hi, z, core):
        return (y_lo * RX + x, (y_hi * RZ + z) * 2 + core)

    z_up = device(x, y_lo, y_hi, (z + 1) % RZ, core)
    z_down = device(x, y_lo, y_hi, (z + RZ - 1) % RZ, core)
    y_far = device(x, y_lo, 1 - y_hi, z, core)
    sib = device(x, y_lo, y_hi, z, 1 - core)
    x_up = device((x + 1) % RX, y_lo, y_hi, z, core)
    x_down = device((x + RX - 1) % RX, y_lo, y_hi, z, core)
    x_far = device((x + RX // 2) % RX, y_lo, y_hi, z, core)
    y_near = device(x, 1 - y_lo, y_hi, z, core)
    partners = (z_up, z_down, y_far, sib, x_up, x_down, x_far, y_near)

    row_copy = pltpu.make_async_copy(rows_hbm, rows_s, in_sem.at[0])
    row_copy_v = pltpu.make_async_copy(rows_hbm, rows_v, in_sem.at[1])
    target_copy = pltpu.make_async_copy(targets_hbm, targets_s, in_sem.at[2])
    a_root = (z % (RZ // 2) == 0) & (core == 0)
    b_root = x % (RX // 2) == 0
    fetch = pltpu.make_async_copy(p_hbm, p_v, p_sem)

    @pl.when(a_root | b_root)
    def _():
        row_copy.start()
        row_copy_v.start()
        fetch.start()

    target_copy.start()

    barrier = pltpu.get_barrier_semaphore()
    for partner in partners:
        pl.semaphore_signal(barrier, inc=1, device_id=partner, device_id_type=MESH)

    for u in range(4):
        a_bufs[u][NA] = jnp.zeros((BLK, BLK), jnp.bfloat16)

    lane = lax.broadcasted_iota(jnp.int32, (8, 128), 1)
    sub = lax.broadcasted_iota(jnp.int32, (8, 128), 0)

    def pick(stored, slots, out):
        last = SLOTS * NCOL - 1
        here = jnp.int32(last)
        chain[last + 1] = here
        for f in range(last, -1, -1):
            here = jnp.where(stored(rows_s[f // NCOL, 0, f % NCOL]), f, here)
            chain[f] = here
        place = chain[0]
        out[0] = place
        for i in range(1, slots):
            place = chain[place + 1]
            out[i] = place

    def before(ones):
        return prefix(ones) - ones

    def row_sum(ones):
        return jnp.sum(ones, axis=1, keepdims=True)

    def prefix(ones):
        total = ones + pltpu.roll(ones, 1, 1)
        total = total + pltpu.roll(total, 2, 1)
        return total + pltpu.roll(total, 4, 1)

    def is_a(row):
        return row >= 0

    def is_b(row):
        return (row >= 0) & (row < NCOL)

    @pl.when(a_root | b_root)
    def _():
        row_copy.wait()

    @pl.when(a_root)
    def _():
        pick(is_a, NA, a_pick)

    def load_ids():
        row_copy_v.wait()
        ids[...] = jnp.full((8, 128), -1, jnp.int32)
        for e in range(SLOTS):
            ids[e:e + 1, 0:NCOL] = rows_v[e]

    def b_table():
        held = ids[...]
        live = is_b(held)
        ones = jnp.where(live, 1, 0)
        sums = row_sum(ones)
        base = jnp.where(sub >= 1, sums[0:1], 0) + jnp.where(sub >= 2, sums[1:2], 0)
        v = x // (RX // 2)
        bm_v[v, 0] = jnp.where(live, held, NCOL)
        bm_v[v, 1] = jnp.where(live, jnp.minimum(before(ones) + base, NB - 1), 0)

    def a_table():
        table = jnp.full((8, 128), NA, jnp.int32)
        wanted = lane // 32 * 8 + sub
        base = jnp.zeros((8, 1), jnp.int32)
        for e in range(SLOTS):
            one = jnp.broadcast_to(ids[e:e + 1, :], (8, 128))
            two = jnp.maximum(one, pltpu.roll(one, 32, 1))
            four = jnp.maximum(two, pltpu.roll(two, 64, 1))
            ones = jnp.where(is_a(four), 1, 0)
            table = jnp.where(four == wanted, jnp.minimum(before(ones) + base, NA), table)
            base = base + row_sum(ones) // 4
        tab_v[z // (RZ // 2)] = table

    @pl.when(a_root | b_root)
    def _():
        fetch.wait()

    for v in range(2):
        @pl.when(a_root & (z == v * (RZ // 2)))
        def _(v=v):
            for i in range(NA):
                a_bufs[v][i] = p_v[a_pick[i]]

    pl.semaphore_wait(barrier, len(partners))

    def remote(src, dst, send, recv, to):
        return pltpu.make_async_remote_copy(
            src_ref=src, dst_ref=dst, send_sem=send, recv_sem=recv, device_id=to, device_id_type=MESH
        )

    def a_steps(u, k):
        flag, v = divmod(u, 2)
        d = (z + RZ - v * (RZ // 2)) % RZ
        mine = pl.ds(core * HALF + k * AB, AB)
        other = pl.ds((1 - core) * HALF + k * AB, AB)
        part, far = a_bufs[u].at[mine], a_bufs[u].at[other]
        even = k % 2 == 0
        up = (d <= 2) | ((d == 3) & even)
        down = (d == 0) | (d >= 6) | ((d == 5) & (k % 2 == 1))
        if flag:
            up, down = up & (k >= EARLY), down & (k >= EARLY)
        out = dict(
            up=(up, remote(part, part, a_send.at[0, u, k], a_recv.at[u, k], z_up)),
            down=(down, remote(part, part, a_send.at[1, u, k], a_recv.at[u, k], z_down)),
            side=(None, remote(part, part, a_ssend.at[u, k], a_srecv.at[u, k], sib)),
        )
        if flag == 0:
            across = a_bufs[u + 2].at[mine]
            out["side"] = ((d != 0) | (core == 0), out["side"][1])
            out["across"] = (
                (d == 0) | (k < EARLY), remote(part, across, a_send.at[2, u, k], a_recv.at[u + 2, k], y_far)
            )
            out["far"] = (
                (d == 0) & (core == 0), remote(far, far, a_ssend.at[u, AC + k], a_recv.at[u, k], sib)
            )
        return out

    def t_steps(u):
        flag, v = divmod(u, 2)
        d = (z + RZ - v * (RZ // 2)) % RZ
        part = tab_v.at[u]
        out = []
        if flag == 0:
            root = (d == 0) & (core == 0)
            out.append((root, remote(part, part, t_sib.at[u], t_recv.at[u], sib)))
        out.append((d <= 3, remote(part, part, t_send.at[0, u], t_recv.at[u], z_up)))
        out.append(((d == 0) | (d >= 6), remote(part, part, t_send.at[1, u], t_recv.at[u], z_down)))
        if flag == 0:
            out.append((d == 0, remote(part, tab_v.at[u + 2], t_send.at[2, u], t_recv.at[u + 2], y_far)))
        return out

    def b_steps(w, k):
        flag, v = divmod(w, 2)
        d = (x + RX - v * (RX // 2)) % RX
        if k is None:
            part, across = bm_v.at[w], bm_v.at[w % 2 + 2]
            send = lambda n: m_send.at[n, w]
            recv = lambda w: m_recv.at[w]
        else:
            part, across = b_buf.at[w, pl.ds(k * BB, BB)], b_buf.at[w % 2 + 2, pl.ds(k * BB, BB)]
            send = lambda n: b_send.at[n, w, k]
            recv = lambda w: b_recv.at[w, k]
        out = []
        if flag == 0:
            out.append((d != 2 if k == 0 else d == 0, remote(part, across, send(3), recv(w + 2), y_near)))
        for n, to in enumerate((x_up, x_down, x_far)):
            if n == 2 or flag == 0 or k != 0:
                out.append((d == 0, remote(part, part, send(n), recv(w), to)))
        return out

    def start(steps):
        for condition, copy in steps:
            if condition is None:
                copy.start()
            else:
                pl.when(condition)(copy.start)

    def finish(steps):
        for condition, copy in steps:
            if condition is None:
                copy.wait_send()
            else:
                pl.when(condition)(copy.wait_send)

    def arrived(buf, sem):
        remote(buf, buf, loc_sem.at[0], sem, sib).wait_recv()

    def loop(body, low=0, high=AC):
        def step(k, _):
            body(k)
            return 0

        lax.fori_loop(low, high, step, 0)

    def mine(u, k):
        return a_bufs[u].at[pl.ds(core * HALF + k * AB, AB)]

    def relay_a(u, k):
        arrived(mine(u, k), a_recv.at[u, k])
        steps = a_steps(u, k)
        steps.pop("far", None)
        start(steps.values())

    def order(i, side):
        base = i // 4 * 4 + i % 2 * 2 + i // 2 % 2
        return base + side * (1 - 2 * (base % 2))

    def side_of(u):
        return ((z + RZ - u % 2 * (RZ // 2)) % RZ + 3) // RZ

    def relay_range(u, low, high):
        side = side_of(u)
        loop(lambda i: relay_a(u, order(i, side)), low, high)

    def at_root(u):
        return z == u * (RZ // 2)

    def relay_own(u, between=None):
        @pl.when(~at_root(u))
        def _():
            if between is None:
                relay_range(u, 0, 6)
            else:
                relay_range(u, 0, 3)
                between()
                relay_range(u, 3, 6)

        @pl.when(at_root(u))
        def _():
            @pl.when(core == 0)
            def _():
                for k in (0, 1, 4, 2, 3, 6, 5, 7):
                    a_steps(u, k)["far"][1].start()

            def send(i):
                a_steps(u, order(i, 0))["up"][1].start()
                a_steps(u, order(i, 1))["down"][1].start()

            def send_across(i):
                @pl.when(core == 1)
                def _():
                    for k in ((0, 1, 4), (2, 3, 6), (5,), (7,))[i]:
                        arrived(mine(u, k), a_recv.at[u, k])

                send(i)
                a_steps(u, order(i + EARLY, 0))["across"][1].start()

            for i in range(EARLY):
                send_across(i)
            loop(send, EARLY, 6)
            loop(lambda k: start([a_steps(u, k)["side"]]))

    def relay_own_late(u):
        @pl.when(~at_root(u))
        def _():
            relay_range(u, 6, 8)

        @pl.when(at_root(u))
        def _():
            def send(i):
                a_steps(u, order(i, 0))["up"][1].start()
                a_steps(u, order(i, 1))["down"][1].start()

            loop(send, 6)
            loop(lambda i: a_steps(u, order(i, 0))["across"][1].start(), 0, EARLY)

    def relay_late(u):
        relay_range(u, EARLY, AC)

    def relay_early(u):
        relay_range(u, 0, EARLY)

    def relay_t(u):
        flag, v = divmod(u, 2)
        if flag == 0:
            @pl.when((z != v * (RZ // 2)) | (core != 0))
            def _():
                arrived(tab_v.at[u], t_recv.at[u])
        else:
            arrived(tab_v.at[u], t_recv.at[u])
        start(t_steps(u))
        pltpu.make_async_copy(tab_v.at[u], tab_s[u], loc_sem.at[u]).start()

    def b_wait(w):
        arrived(bm_v.at[w], m_recv.at[w])
        for k in range(BC):
            def wait(k=k):
                arrived(b_buf.at[w, pl.ds(k * BB, BB)], b_recv.at[w, k])

            if w < 2 and k == 0:
                pl.when(b_distance(w) == 2)(wait)
            else:
                wait()

    def b_distance(w):
        return (x + RX - (w % 2) * (RX // 2)) % RX

    def send_b(w):
        @pl.when(b_distance(w) == 0)
        def _():
            for k in range(BC):
                if w >= 2:
                    arrived(b_buf.at[w, pl.ds(k * BB, BB)], b_recv.at[w, k])
                start(b_steps(w, k)[:-1])
            for k in range(BC):
                start(b_steps(w, k)[-1:])
            if w >= 2:
                arrived(bm_v.at[w], m_recv.at[w])
                start(b_steps(w, None))

    def b_begin():
        @pl.when(b_root)
        def _():
            pick(is_b, NB, b_pick)
            for i in range(NB):
                b_buf[x // (RX // 2), i] = p_v[b_pick[i]]

        for w in (0, 1):
            send_b(w)

    pl.when(~a_root)(b_begin)

    def b_own_tables():
        @pl.when(b_root)
        def _():
            b_table()
            for w in (0, 1):
                pl.when(b_distance(w) == 0)(lambda w=w: start(b_steps(w, None)))

    def b_peers():
        for w in (0, 1):
            @pl.when(b_distance(w) % 2 == 1)
            def _(w=w):
                arrived(b_buf.at[w, pl.ds(0, BB)], b_recv.at[w, 0])
                start(b_steps(w, 0)[:1])

        for w in (2, 3):
            send_b(w)

    def b_ready():
        for w in range(4):
            pl.when(b_distance(w) != 0)(functools.partial(b_wait, w))
        to_smem = pltpu.make_async_copy(bm_v, bm_s, bm_sem)
        to_smem.start()
        to_smem.wait()

    def a_ready(u):
        pltpu.make_async_copy(tab_v.at[u], tab_s[u], loc_sem.at[u]).wait()

        def wait(k):
            arrived(a_bufs[u].at[pl.ds((1 - core) * HALF + k * AB, AB)], a_srecv.at[u, k])

        if u < 2:
            @pl.when((z != u * (RZ // 2)) | (core != 0))
            def _():
                loop(wait)
        else:
            loop(wait)

    def column(pair, j, first):
        places = []
        for s in range(SLOTS):
            target = targets_s[s, 0, j]
            places.append((target % 8, target // 8 * 32))
        left, right = [], []
        for u in pair:
            flag, v = divmod(u, 2)
            w = (flag + y_hi + y_lo) % 2 * 2 + v
            panel, table = a_bufs[u], tab_s[u]
            for e in range(SLOTS):
                at = bm_s[w, 0, e, j]
                right.append(b_buf[w, bm_s[w, 1, e, j]])
                left.append([panel[table[low, high + at]] for low, high in places])
        right = jnp.concatenate(right, axis=0)
        for s in range(SLOTS):
            piece = jnp.dot(
                jnp.concatenate([blocks[s] for blocks in left], axis=1), right, preferred_element_type=jnp.float32
            )
            acc[s, j] = piece if first else acc[s, j] + piece

    target_copy.wait()
    def a_sent(u):
        finish(t_steps(u))
        loop(lambda k: finish(a_steps(u, k).values()))

    def columns(pair, first):
        def step(i):
            for j in (i * 2, i * 2 + 1):
                column(pair, j, first)

        loop(step, 0, NCOL // 2)

    for near in (0, 1):
        @pl.when((z % 4 != 2) & ((z + 2) // 4 % 2 == near))
        def _(near=near):
            far = 1 - near
            relay_own(near)
            pl.when(a_root)(b_begin)
            pl.when(a_root | b_root)(load_ids)
            pl.when(a_root)(a_table)
            relay_t(near)
            b_own_tables()
            pl.when(z % 4 != 0)(b_peers)
            relay_late(near + 2)
            relay_t(near + 2)
            relay_own_late(near)
            pl.when(z % 4 == 0)(b_peers)
            relay_early(near + 2)
            relay_own(far)
            relay_t(far)

            @pl.when(z % 4 == 0)
            def _():
                relay_own_late(far)

            @pl.when(z % 4 != 0)
            def _():
                relay_late(far + 2)
                relay_t(far + 2)

            a_sent(near)
            a_sent(near + 2)
            b_ready()
            a_ready(near)
            a_ready(near + 2)

            @pl.when(z % 4 == 0)
            def _():
                def step(i):
                    column((near, near + 2), i * 2, True)
                    column((near, near + 2), i * 2 + 1, True)
                    relay_a(far + 2, order(i + EARLY, side_of(far)))

                loop(step, 0, EARLY)
                relay_t(far + 2)
                relay_early(far + 2)

            @pl.when(z % 4 != 0)
            def _():
                def step(i):
                    relay_a(far + 2, order(i, side_of(far)))

                    @pl.when(i >= 2)
                    def _():
                        relay_a(far, order(i + EARLY, side_of(far)))

                    column((near, near + 2), i * 2, True)
                    column((near, near + 2), i * 2 + 1, True)

                loop(step, 0, EARLY)

            a_ready(far)
            a_ready(far + 2)

            columns((far, far + 2), False)
            a_sent(far)
            a_sent(far + 2)

    @pl.when(z % 4 == 2)
    def _():
        @pl.when(b_root)
        def _():
            load_ids()

        b_own_tables()

        def both(u, low, high):
            def step(i):
                relay_a(u, order(i, side_of(0)))
                relay_a(u + 1, order(i, side_of(1)))

            loop(step, low, high)

        both(0, 0, 3)
        b_peers()
        both(0, 3, 6)
        relay_t(0)
        relay_t(1)
        both(2, EARLY, AC)
        relay_t(2)
        relay_t(3)
        both(0, 6, AC)
        both(2, 0, EARLY)
        for u in range(4):
            a_sent(u)
        b_ready()
        a_ready(0)
        a_ready(2)
        columns((0, 2), True)
        a_ready(1)
        a_ready(3)

        columns((1, 3), False)

    for w in range(4):
        finish(b_steps(w, None))
        for k in range(BC):
            finish(b_steps(w, k))


def local(p_blocks, p_rows, c_rows):
    blocks = p_blocks.reshape(SLOTS * NCOL, BLK, BLK)
    rows, targets = p_rows.transpose(1, 0, 2), c_rows.transpose(1, 0, 2)
    dma = pltpu.SemaphoreType.DMA
    out = pl.pallas_call(
        kernel,
        out_shape=pltpu.VMEM((SLOTS, NCOL, BLK, BLK), jnp.float32),
        in_specs=[
            pl.BlockSpec(memory_space=pl.ANY),
            pl.BlockSpec(memory_space=pl.ANY),
            pl.BlockSpec(memory_space=pl.ANY),
        ],
        out_specs=pl.BlockSpec(memory_space=pltpu.VMEM),
        scratch_shapes=[pltpu.VMEM((NA + 1, BLK, BLK), jnp.bfloat16)] * 4
        + [pltpu.SMEM((8, 128), jnp.int32)] * 4
        + [
            pltpu.VMEM((4, NB, BLK, BLK), jnp.bfloat16),
            pltpu.VMEM((4, 8, 128), jnp.int32),
            pltpu.VMEM((4, 2, 8, 128), jnp.int32),
            pltpu.SMEM((4, 2, 8, 128), jnp.int32),
            pltpu.VMEM((SLOTS * NCOL, BLK, BLK), jnp.bfloat16),
            pltpu.VMEM((8, 128), jnp.int32),
            pltpu.SMEM((NA,), jnp.int32),
            pltpu.SMEM((NB,), jnp.int32),
            dma,
            dma((4, AC)), dma((4, AC)), dma((4, 2 * AC)), dma((3, 4, AC)),
            dma((4,)), dma((3, 4)), dma((4,)),
            dma((4, BC)), dma((4, 4, BC)), dma((4,)), dma((4, 4)),
            dma((4,)), dma,
            pltpu.SMEM((SLOTS, 1, NCOL), jnp.int32),
            pltpu.SMEM((SLOTS, 1, NCOL), jnp.int32),
            pltpu.VMEM((SLOTS, 1, NCOL), jnp.int32),
            dma((3,)),
            pltpu.SMEM((SLOTS * NCOL + 1,), jnp.int32),
        ],
        compiler_params=pltpu.CompilerParams(
            collective_id=0, has_side_effects=True, vmem_limit_bytes=(65536 - 4096) * 1024
        ),
        name="panels",
    )(blocks, rows, targets)
    return out[None]


def solution(mesh):
    placed = (P("row", None, "col", None, None), P("row", None, "col"), P("row", None, "col"))
    return jax.shard_map(
        local,
        mesh=mesh,
        in_specs=placed,
        out_specs=P("row", None, "col", None, None),
        check_vma=False,
    )
```

```python
import functools

import jax
import jax.numpy as jnp
from jax import lax
from jax.experimental import pallas as pl
from jax.experimental.pallas import tpu as pltpu
from jax.sharding import PartitionSpec as P

MESH = pl.DeviceIdType.MESH
BLK = 128
NCOL = 8
SLOTS = 3
NA = 16
NB = 6
HALF = NA // 2
AC = 8
AB = HALF // AC
EARLY = AC // 2
BC = 2
BB = NB // BC
RX, RZ = 4, 8


def kernel(p_hbm, rows_hbm, targets_hbm, acc, *scratch):
    a_bufs = scratch[0:4]
    tab_s = scratch[4:8]
    (b_buf, tab_v, bm_v, bm_s, p_v, ids, a_pick, b_pick, p_sem,
     a_recv, a_srecv, a_ssend, a_send, t_recv, t_send, t_sib,
     b_recv, b_send, m_recv, m_send, loc_sem, bm_sem, rows_s, targets_s, rows_v, in_sem, chain) = scratch[8:]

    r, c = lax.axis_index("row"), lax.axis_index("col")
    x, y_lo = r % RX, r // RX
    core, z, y_hi = c % 2, (c // 2) % RZ, c // (2 * RZ)

    def device(x, y_lo, y_hi, z, core):
        return (y_lo * RX + x, (y_hi * RZ + z) * 2 + core)

    z_up = device(x, y_lo, y_hi, (z + 1) % RZ, core)
    z_down = device(x, y_lo, y_hi, (z + RZ - 1) % RZ, core)
    y_far = device(x, y_lo, 1 - y_hi, z, core)
    sib = device(x, y_lo, y_hi, z, 1 - core)
    x_up = device((x + 1) % RX, y_lo, y_hi, z, core)
    x_down = device((x + RX - 1) % RX, y_lo, y_hi, z, core)
    x_far = device((x + RX // 2) % RX, y_lo, y_hi, z, core)
    y_near = device(x, 1 - y_lo, y_hi, z, core)
    partners = (z_up, z_down, y_far, sib, x_up, x_down, x_far, y_near)

    barrier = pltpu.get_barrier_semaphore()
    for partner in partners:
        pl.semaphore_signal(barrier, inc=1, device_id=partner, device_id_type=MESH)

    row_copy = pltpu.make_async_copy(rows_hbm, rows_s, in_sem.at[0])
    row_copy_v = pltpu.make_async_copy(rows_hbm, rows_v, in_sem.at[1])
    target_copy = pltpu.make_async_copy(targets_hbm, targets_s, in_sem.at[2])
    a_root = (z % (RZ // 2) == 0) & (core == 0)
    b_root = x % (RX // 2) == 0
    fetch = pltpu.make_async_copy(p_hbm, p_v, p_sem)

    @pl.when(a_root | b_root)
    def _():
        row_copy.start()
        row_copy_v.start()
        fetch.start()

    target_copy.start()

    for u in range(4):
        a_bufs[u][NA] = jnp.zeros((BLK, BLK), jnp.bfloat16)

    lane = lax.broadcasted_iota(jnp.int32, (8, 128), 1)
    sub = lax.broadcasted_iota(jnp.int32, (8, 128), 0)

    def pick(stored, slots, out):
        last = SLOTS * NCOL - 1
        here = jnp.int32(last)
        chain[last + 1] = here
        for f in range(last, -1, -1):
            here = jnp.where(stored(rows_s[f // NCOL, 0, f % NCOL]), f, here)
            chain[f] = here
        place = chain[0]
        out[0] = place
        for i in range(1, slots):
            place = chain[place + 1]
            out[i] = place

    def before(ones):
        return prefix(ones) - ones

    def row_sum(ones):
        return jnp.sum(ones, axis=1, keepdims=True)

    def prefix(ones):
        total = ones + pltpu.roll(ones, 1, 1)
        total = total + pltpu.roll(total, 2, 1)
        return total + pltpu.roll(total, 4, 1)

    def is_a(row):
        return row >= 0

    def is_b(row):
        return (row >= 0) & (row < NCOL)

    @pl.when(a_root | b_root)
    def _():
        row_copy.wait()

    @pl.when(a_root)
    def _():
        pick(is_a, NA, a_pick)

    def load_ids():
        row_copy_v.wait()
        ids[...] = jnp.full((8, 128), -1, jnp.int32)
        for e in range(SLOTS):
            ids[e:e + 1, 0:NCOL] = rows_v[e]

    def b_table():
        held = ids[...]
        live = is_b(held)
        ones = jnp.where(live, 1, 0)
        sums = row_sum(ones)
        base = jnp.where(sub >= 1, sums[0:1], 0) + jnp.where(sub >= 2, sums[1:2], 0)
        v = x // (RX // 2)
        bm_v[v, 0] = jnp.where(live, held, NCOL)
        bm_v[v, 1] = jnp.where(live, jnp.minimum(before(ones) + base, NB - 1), 0)

    def a_table():
        table = jnp.full((8, 128), NA, jnp.int32)
        wanted = lane // 32 * 8 + sub
        base = jnp.zeros((8, 1), jnp.int32)
        for e in range(SLOTS):
            one = jnp.broadcast_to(ids[e:e + 1, :], (8, 128))
            two = jnp.maximum(one, pltpu.roll(one, 32, 1))
            four = jnp.maximum(two, pltpu.roll(two, 64, 1))
            ones = jnp.where(is_a(four), 1, 0)
            table = jnp.where(four == wanted, jnp.minimum(before(ones) + base, NA), table)
            base = base + row_sum(ones) // 4
        tab_v[z // (RZ // 2)] = table

    @pl.when(a_root | b_root)
    def _():
        fetch.wait()

    for v in range(2):
        @pl.when(a_root & (z == v * (RZ // 2)))
        def _(v=v):
            for i in range(NA):
                a_bufs[v][i] = p_v[a_pick[i]]

    pl.semaphore_wait(barrier, len(partners))

    def remote(src, dst, send, recv, to):
        return pltpu.make_async_remote_copy(
            src_ref=src, dst_ref=dst, send_sem=send, recv_sem=recv, device_id=to, device_id_type=MESH
        )

    def a_steps(u, k):
        flag, v = divmod(u, 2)
        d = (z + RZ - v * (RZ // 2)) % RZ
        mine = pl.ds(core * HALF + k * AB, AB)
        other = pl.ds((1 - core) * HALF + k * AB, AB)
        part, far = a_bufs[u].at[mine], a_bufs[u].at[other]
        even = k % 2 == 0
        up = (d <= 2) | ((d == 3) & even)
        down = (d == 0) | (d >= 6) | ((d == 5) & (k % 2 == 1))
        if flag:
            up, down = up & (k >= EARLY), down & (k >= EARLY)
        out = dict(
            up=(up, remote(part, part, a_send.at[0, u, k], a_recv.at[u, k], z_up)),
            down=(down, remote(part, part, a_send.at[1, u, k], a_recv.at[u, k], z_down)),
            side=(None, remote(part, part, a_ssend.at[u, k], a_srecv.at[u, k], sib)),
        )
        if flag == 0:
            across = a_bufs[u + 2].at[mine]
            out["side"] = ((d != 0) | (core == 0), out["side"][1])
            out["across"] = (
                (d == 0) | (k < EARLY), remote(part, across, a_send.at[2, u, k], a_recv.at[u + 2, k], y_far)
            )
            out["far"] = (
                (d == 0) & (core == 0), remote(far, far, a_ssend.at[u, AC + k], a_recv.at[u, k], sib)
            )
        return out

    def t_steps(u):
        flag, v = divmod(u, 2)
        d = (z + RZ - v * (RZ // 2)) % RZ
        part = tab_v.at[u]
        out = []
        if flag == 0:
            root = (d == 0) & (core == 0)
            out.append((root, remote(part, part, t_sib.at[u], t_recv.at[u], sib)))
        out.append((d <= 3, remote(part, part, t_send.at[0, u], t_recv.at[u], z_up)))
        out.append(((d == 0) | (d >= 6), remote(part, part, t_send.at[1, u], t_recv.at[u], z_down)))
        if flag == 0:
            out.append((d == 0, remote(part, tab_v.at[u + 2], t_send.at[2, u], t_recv.at[u + 2], y_far)))
        return out

    def b_steps(w, k):
        flag, v = divmod(w, 2)
        d = (x + RX - v * (RX // 2)) % RX
        if k is None:
            part, across = bm_v.at[w], bm_v.at[w % 2 + 2]
            send = lambda n: m_send.at[n, w]
            recv = lambda w: m_recv.at[w]
        else:
            part, across = b_buf.at[w, pl.ds(k * BB, BB)], b_buf.at[w % 2 + 2, pl.ds(k * BB, BB)]
            send = lambda n: b_send.at[n, w, k]
            recv = lambda w: b_recv.at[w, k]
        out = []
        if flag == 0:
            out.append((d != 2 if k == 0 else d == 0, remote(part, across, send(3), recv(w + 2), y_near)))
        for n, to in enumerate((x_up, x_down, x_far)):
            if n == 2 or flag == 0 or k != 0:
                out.append((d == 0, remote(part, part, send(n), recv(w), to)))
        return out

    def start(steps):
        for condition, copy in steps:
            if condition is None:
                copy.start()
            else:
                pl.when(condition)(copy.start)

    def finish(steps):
        for condition, copy in steps:
            if condition is None:
                copy.wait_send()
            else:
                pl.when(condition)(copy.wait_send)

    def arrived(buf, sem):
        remote(buf, buf, loc_sem.at[0], sem, sib).wait_recv()

    def loop(body, low=0, high=AC):
        def step(k, _):
            body(k)
            return 0

        lax.fori_loop(low, high, step, 0)

    def mine(u, k):
        return a_bufs[u].at[pl.ds(core * HALF + k * AB, AB)]

    def relay_a(u, k):
        arrived(mine(u, k), a_recv.at[u, k])
        steps = a_steps(u, k)
        steps.pop("far", None)
        start(steps.values())

    def order(i, side):
        base = i // 4 * 4 + i % 2 * 2 + i // 2 % 2
        return base + side * (1 - 2 * (base % 2))

    def side_of(u):
        return ((z + RZ - u % 2 * (RZ // 2)) % RZ + 3) // RZ

    def relay_range(u, low, high):
        side = side_of(u)
        loop(lambda i: relay_a(u, order(i, side)), low, high)

    def at_root(u):
        return z == u * (RZ // 2)

    def relay_own(u, between=None):
        @pl.when(~at_root(u))
        def _():
            if between is None:
                relay_range(u, 0, 6)
            else:
                relay_range(u, 0, 3)
                between()
                relay_range(u, 3, 6)

        @pl.when(at_root(u))
        def _():
            @pl.when(core == 0)
            def _():
                loop(lambda k: a_steps(u, k)["far"][1].start())

            @pl.when(core == 1)
            def _():
                loop(lambda k: arrived(mine(u, k), a_recv.at[u, k]))

            def send(i):
                a_steps(u, order(i, 0))["up"][1].start()
                a_steps(u, order(i, 1))["down"][1].start()

            def send_across(i):
                send(i)
                a_steps(u, order(i + EARLY, 0))["across"][1].start()

            loop(send_across, 0, EARLY)
            loop(send, EARLY, 6)
            loop(lambda k: start([a_steps(u, k)["side"]]))

    def relay_own_late(u):
        @pl.when(~at_root(u))
        def _():
            relay_range(u, 6, 8)

        @pl.when(at_root(u))
        def _():
            def send(i):
                a_steps(u, order(i, 0))["up"][1].start()
                a_steps(u, order(i, 1))["down"][1].start()

            loop(send, 6)
            loop(lambda i: a_steps(u, order(i, 0))["across"][1].start(), 0, EARLY)

    def relay_late(u):
        relay_range(u, EARLY, AC)

    def relay_early(u):
        relay_range(u, 0, EARLY)

    def relay_t(u):
        flag, v = divmod(u, 2)
        if flag == 0:
            @pl.when((z != v * (RZ // 2)) | (core != 0))
            def _():
                arrived(tab_v.at[u], t_recv.at[u])
        else:
            arrived(tab_v.at[u], t_recv.at[u])
        start(t_steps(u))
        pltpu.make_async_copy(tab_v.at[u], tab_s[u], loc_sem.at[u]).start()

    def b_wait(w):
        arrived(bm_v.at[w], m_recv.at[w])
        for k in range(BC):
            def wait(k=k):
                arrived(b_buf.at[w, pl.ds(k * BB, BB)], b_recv.at[w, k])

            if w < 2 and k == 0:
                pl.when(b_distance(w) == 2)(wait)
            else:
                wait()

    def b_distance(w):
        return (x + RX - (w % 2) * (RX // 2)) % RX

    def send_b(w):
        @pl.when(b_distance(w) == 0)
        def _():
            for k in range(BC):
                if w >= 2:
                    arrived(b_buf.at[w, pl.ds(k * BB, BB)], b_recv.at[w, k])
                start(b_steps(w, k)[:-1])
            for k in range(BC):
                start(b_steps(w, k)[-1:])
            if w >= 2:
                arrived(bm_v.at[w], m_recv.at[w])
                start(b_steps(w, None))

    def b_begin():
        @pl.when(b_root)
        def _():
            pick(is_b, NB, b_pick)
            for i in range(NB):
                b_buf[x // (RX // 2), i] = p_v[b_pick[i]]

        for w in (0, 1):
            send_b(w)

    pl.when(~a_root)(b_begin)

    def b_own_tables():
        @pl.when(b_root)
        def _():
            b_table()
            for w in (0, 1):
                pl.when(b_distance(w) == 0)(lambda w=w: start(b_steps(w, None)))

    def b_peers():
        for w in (0, 1):
            @pl.when(b_distance(w) % 2 == 1)
            def _(w=w):
                arrived(b_buf.at[w, pl.ds(0, BB)], b_recv.at[w, 0])
                start(b_steps(w, 0)[:1])

        for w in (2, 3):
            send_b(w)

    def b_ready():
        for w in range(4):
            pl.when(b_distance(w) != 0)(functools.partial(b_wait, w))
        to_smem = pltpu.make_async_copy(bm_v, bm_s, bm_sem)
        to_smem.start()
        to_smem.wait()

    def a_ready(u):
        pltpu.make_async_copy(tab_v.at[u], tab_s[u], loc_sem.at[u]).wait()

        def wait(k):
            arrived(a_bufs[u].at[pl.ds((1 - core) * HALF + k * AB, AB)], a_srecv.at[u, k])

        if u < 2:
            @pl.when((z != u * (RZ // 2)) | (core != 0))
            def _():
                loop(wait)
        else:
            loop(wait)

    def column(pair, j, first):
        places = []
        for s in range(SLOTS):
            target = targets_s[s, 0, j]
            places.append((target % 8, target // 8 * 32))
        left, right = [], []
        for u in pair:
            flag, v = divmod(u, 2)
            w = (flag + y_hi + y_lo) % 2 * 2 + v
            panel, table = a_bufs[u], tab_s[u]
            for e in range(SLOTS):
                at = bm_s[w, 0, e, j]
                right.append(b_buf[w, bm_s[w, 1, e, j]])
                left.append([panel[table[low, high + at]] for low, high in places])
        right = jnp.concatenate(right, axis=0)
        for s in range(SLOTS):
            piece = jnp.dot(
                jnp.concatenate([blocks[s] for blocks in left], axis=1), right, preferred_element_type=jnp.float32
            )
            acc[s, j] = piece if first else acc[s, j] + piece

    target_copy.wait()
    def columns(pair, first):
        def step(i):
            for part in range(4):
                column(pair, i * 4 + part, first)

        loop(step, 0, NCOL // 4)

    for near in (0, 1):
        @pl.when((z % 4 != 2) & ((z + 2) // 4 % 2 == near))
        def _(near=near):
            far = 1 - near
            relay_own(near)
            pl.when(a_root)(b_begin)
            pl.when(a_root | b_root)(load_ids)
            pl.when(a_root)(a_table)
            relay_t(near)
            b_own_tables()
            pl.when(z % 4 != 0)(b_peers)
            relay_late(near + 2)
            relay_t(near + 2)
            relay_own_late(near)
            pl.when(z % 4 == 0)(b_peers)
            relay_early(near + 2)
            relay_own(far)
            relay_t(far)

            @pl.when(z % 4 == 0)
            def _():
                relay_own_late(far)

            @pl.when(z % 4 != 0)
            def _():
                relay_late(far + 2)
                relay_t(far + 2)

            b_ready()
            a_ready(near)
            a_ready(near + 2)

            @pl.when(z % 4 == 0)
            def _():
                def step(i):
                    column((near, near + 2), i * 2, True)
                    column((near, near + 2), i * 2 + 1, True)
                    relay_a(far + 2, order(i + EARLY, side_of(far)))

                loop(step, 0, EARLY)
                relay_t(far + 2)
                relay_early(far + 2)

            @pl.when(z % 4 != 0)
            def _():
                def step(i):
                    relay_a(far + 2, order(i, side_of(far)))

                    @pl.when(i >= 2)
                    def _():
                        relay_a(far, order(i + EARLY, side_of(far)))

                    column((near, near + 2), i * 2, True)
                    column((near, near + 2), i * 2 + 1, True)

                loop(step, 0, EARLY)

            a_ready(far)
            a_ready(far + 2)

            columns((far, far + 2), False)

    @pl.when(z % 4 == 2)
    def _():
        @pl.when(b_root)
        def _():
            load_ids()

        b_own_tables()

        def both(u, low, high):
            def step(i):
                relay_a(u, order(i, side_of(0)))
                relay_a(u + 1, order(i, side_of(1)))

            loop(step, low, high)

        both(0, 0, 3)
        b_peers()
        both(0, 3, 6)
        relay_t(0)
        relay_t(1)
        both(2, EARLY, AC)
        relay_t(2)
        relay_t(3)
        both(0, 6, AC)
        both(2, 0, EARLY)
        b_ready()
        a_ready(0)
        a_ready(2)
        columns((0, 2), True)
        a_ready(1)
        a_ready(3)

        columns((1, 3), False)

    for u in range(4):
        finish(t_steps(u))
        loop(lambda k: finish(a_steps(u, k).values()))
    for w in range(4):
        finish(b_steps(w, None))
        for k in range(BC):
            finish(b_steps(w, k))


def local(p_blocks, p_rows, c_rows):
    blocks = p_blocks.reshape(SLOTS * NCOL, BLK, BLK)
    rows, targets = p_rows.transpose(1, 0, 2), c_rows.transpose(1, 0, 2)
    dma = pltpu.SemaphoreType.DMA
    out = pl.pallas_call(
        kernel,
        out_shape=pltpu.VMEM((SLOTS, NCOL, BLK, BLK), jnp.float32),
        in_specs=[
            pl.BlockSpec(memory_space=pl.ANY),
            pl.BlockSpec(memory_space=pl.ANY),
            pl.BlockSpec(memory_space=pl.ANY),
        ],
        out_specs=pl.BlockSpec(memory_space=pltpu.VMEM),
        scratch_shapes=[pltpu.VMEM((NA + 1, BLK, BLK), jnp.bfloat16)] * 4
        + [pltpu.SMEM((8, 128), jnp.int32)] * 4
        + [
            pltpu.VMEM((4, NB, BLK, BLK), jnp.bfloat16),
            pltpu.VMEM((4, 8, 128), jnp.int32),
            pltpu.VMEM((4, 2, 8, 128), jnp.int32),
            pltpu.SMEM((4, 2, 8, 128), jnp.int32),
            pltpu.VMEM((SLOTS * NCOL, BLK, BLK), jnp.bfloat16),
            pltpu.VMEM((8, 128), jnp.int32),
            pltpu.SMEM((NA,), jnp.int32),
            pltpu.SMEM((NB,), jnp.int32),
            dma,
            dma((4, AC)), dma((4, AC)), dma((4, 2 * AC)), dma((3, 4, AC)),
            dma((4,)), dma((3, 4)), dma((4,)),
            dma((4, BC)), dma((4, 4, BC)), dma((4,)), dma((4, 4)),
            dma((4,)), dma,
            pltpu.SMEM((SLOTS, 1, NCOL), jnp.int32),
            pltpu.SMEM((SLOTS, 1, NCOL), jnp.int32),
            pltpu.VMEM((SLOTS, 1, NCOL), jnp.int32),
            dma((3,)),
            pltpu.SMEM((SLOTS * NCOL + 1,), jnp.int32),
        ],
        compiler_params=pltpu.CompilerParams(
            collective_id=0, has_side_effects=True, vmem_limit_bytes=(65536 - 4096) * 1024
        ),
        name="panels",
    )(blocks, rows, targets)
    return out[None]


def solution(mesh):
    placed = (P("row", None, "col", None, None), P("row", None, "col"), P("row", None, "col"))
    return jax.shard_map(
        local,
        mesh=mesh,
        in_specs=placed,
        out_specs=P("row", None, "col", None, None),
        check_vma=False,
    )
```
